256 devices in a mesh: dp: 8 (over z), pack: 32 (over x, y, core).
Axes of the slice: x: 4, y: 4, z: 8, core: 2. Of those that a mesh axis runs over, the one named last changes fastest.
Arguments:
- enc_keys: bfloat16 [65536, 4096], P(('dp', 'pack')), may hold values from -4 to 4
- enc_values: bfloat16 [65536, 4096], P(('dp', 'pack')), may hold values from -6 to 6
- dec_queries: bfloat16 [32768, 4096], P(('dp', 'pack')), may hold values from -4 to 4
- cotangent: bfloat16 [32768, 4096], P(('dp', 'pack')), may hold values from -6 to 6
- input_lengths: int32 [8, 64], P('dp'), may hold values from 16 to 240, as said below
- target_lengths: int32 [8, 64], P('dp'), may hold values from 8 to 120, as said below
- enc_pack: int32 [8, 64], P('dp'), may hold values from 0 to 31, as said below
- dec_pack: int32 [8, 64], P('dp'), may hold values from 0 to 31, as said below
- task_group: int32 [8, 64, 1], P('dp'), may hold values from 0 to 15
- dro_weights: int32 [16], replicated, may hold values from 1 to 8
Outputs:
- queries_gradient: bfloat16 [32768, 4096], P(('dp', 'pack'))
- keys_gradient: bfloat16 [65536, 4096], P(('dp', 'pack'))
- values_gradient: bfloat16 [65536, 4096], P(('dp', 'pack'))
- group_loss: float32 [16], replicated
The draws below stay inside these ranges and needn't reach their ends.
Inputs may be any that keep to these rules, and one draw needn't show every extreme that they name: `input_lengths`: within one data group, the input lengths of the examples of one encoder pack add up to exactly 256; every length is a multiple of 16. `target_lengths`: within one data group, the target lengths of the examples of one decoder pack add up to exactly 128; every length is a multiple of 8. `enc_pack`: within one data group, every encoder pack holds exactly 2 examples. `dec_pack`: within one data group, every decoder pack holds exactly 2 examples.
All inputs are finite; a program needn't handle non-finite values.
Results may differ from the reference program's by a relative error of at most 0.012.
The reference program's roundings to bfloat16 on the way (of `attention_low`, `attended`, `upstream` and `scores_gradient`) count: a program that leaves them out, or rounds other values in their place, can miss the bound.
Values may be sent and summed in bfloat16 or wider, within the bound.
A program may use at most 128 MiB of HBM per device.

```python
import jax
import jax.numpy as jnp
from jax import lax

HEADS = 64
HEAD_DIM = 64
D = 4096
ENC_DEV = 256
DEC_DEV = 128
EX_DEV = 2
GROUPS = 16
ENC_SLOT = 240
DEC_SLOT = 120
EX_GRP = 64
ENC_TOKENS = 65536
DEC_TOKENS = 32768
N_DP = 8
N_PACK = 32


def assignment(key, offset_salt):
    key = jax.random.fold_in(key, offset_salt)
    shuffled = jax.vmap(lambda one_key: jax.random.permutation(one_key, EX_DEV * N_PACK))(jax.random.split(key, N_DP))
    shuffled = shuffled.astype(jnp.int32)
    return (shuffled // EX_DEV, shuffled % EX_DEV)


def pack_pieces(key, per_pack, step_size):
    base = per_pack // EX_DEV
    reach = base // step_size - 1
    pair_count = EX_DEV // 2
    shifts = jax.random.randint(key, (N_DP, N_PACK, pair_count), -reach, reach + 1).astype(jnp.int32)
    forced_pack = jax.random.randint(jax.random.fold_in(key, 7), (N_DP, 1), 0, N_PACK)
    forced = (jnp.arange(N_PACK, dtype=jnp.int32)[None, :] == forced_pack)[:, :, None] & (jnp.arange(pair_count, dtype=jnp.int32)[None, None, :] == 0)
    shifts = jnp.where(forced, reach, shifts)
    longer = base + shifts * step_size
    shorter = base - shifts * step_size
    return jnp.stack([longer, shorter], axis=-1).reshape(N_DP, N_PACK, EX_DEV).astype(jnp.int32)


def lengths_for(pieces, pack_index, slot_index):
    flat_pieces = pieces.reshape(N_DP, N_PACK * EX_DEV)
    return jnp.take_along_axis(flat_pieces, pack_index * EX_DEV + slot_index, axis=1).astype(jnp.int32)


def draw_input_lengths(key, part):
    pack_index, slot_index = assignment(key, 11)
    key = jax.random.fold_in(key, 3)
    return lengths_for(pack_pieces(key, ENC_DEV, 16), pack_index, slot_index)


def draw_target_lengths(key, part):
    pack_index, slot_index = assignment(key, 21)
    key = jax.random.fold_in(key, 4)
    return lengths_for(pack_pieces(key, DEC_DEV, 8), pack_index, slot_index)


def draw_enc_pack(key, part):
    pack_index, slot_index = assignment(key, 11)
    return pack_index


def draw_dec_pack(key, part):
    pack_index, slot_index = assignment(key, 21)
    return pack_index


def draw_enc_keys(key, part):
    key = jax.random.fold_in(key, 5)
    row_total = ENC_DEV * N_PACK * N_DP
    sample = jnp.clip(0.35 * jax.random.normal(key, (row_total, D), jnp.float32), -4.0, 4.0)
    return jnp.clip(sample, -4.0, 4.0).astype(jnp.bfloat16)


def draw_dec_queries(key, part):
    key = jax.random.fold_in(key, 6)
    row_total = DEC_DEV * N_PACK * N_DP
    sample = jnp.clip(0.35 * jax.random.normal(key, (row_total, D), jnp.float32), -4.0, 4.0)
    return sample.astype(jnp.bfloat16)


def with_ends(values, stream_key, smallest, top_value):
    shape = values.shape
    place = [jax.random.randint(jax.random.fold_in(stream_key, axis), (), 0, shape[axis]) for axis in range(len(shape))]
    values = values.at[tuple(place)].set(smallest)
    longest = shape.index(max(shape))
    place[longest] = (place[longest] + 1) % shape[longest]
    return values.at[tuple(place)].set(top_value)


def level_of(rng, dims, cuts, least, high):
    loudness, own = 1.0, jax.random.fold_in(rng, 6)
    for axis_at, parts in cuts:
        steps = jnp.exp(jax.random.uniform(jax.random.fold_in(own, axis_at), (parts,), jnp.float32, least / len(cuts), high / len(cuts)))
        loudness = loudness * jnp.repeat(steps, dims[axis_at] // parts).reshape([-1 if axis == axis_at else 1 for axis in range(len(dims))])
    return loudness


def picks_of(own_key, rows, number_of, top, lift):
    order = jax.random.permutation(jax.random.fold_in(own_key, 1), number_of)
    boost = order
    for power in range(3):
        boost = boost * boost // number_of
    boost = boost * lift // number_of
    tickets = jax.random.randint(jax.random.fold_in(own_key, 2), (rows, number_of), 0, 4096) + boost
    fixed_rows = jax.random.permutation(jax.random.fold_in(own_key, 3), rows)[jnp.arange(number_of) % rows]
    tickets = jnp.where(jnp.arange(rows)[:, None] == fixed_rows[None, :], 1 << 14, tickets)
    merit = tickets * number_of + jnp.arange(number_of)
    return lax.top_k(merit.astype(jnp.int32), top)[1].astype(jnp.int32)


def bell_draw(rng, dims, width, limit, cuts=(), kind=jnp.bfloat16):
    loudness = level_of(rng, dims, cuts, -0.22, 0.18) if cuts else 1.0
    result = jax.random.normal(rng, dims, jnp.float32) * width * loudness
    return jnp.minimum(jnp.maximum(result, -limit), limit).astype(kind)


def setup_inputs(seed: int = 0) -> dict:
    arg_keys = jax.random.split(jax.random.key(seed), 11)
    enc_keys = draw_enc_keys(jax.random.fold_in(arg_keys[10], 71), 0)
    enc_values = bell_draw(arg_keys[1], (ENC_TOKENS, D), 1.0, 6.0, ((0, 256),))
    dec_queries = draw_dec_queries(jax.random.fold_in(arg_keys[10], 71), 0)
    cotangent = bell_draw(arg_keys[3], (DEC_TOKENS, D), 1.0, 6.0, ((0, 256),))
    input_lengths = draw_input_lengths(jax.random.fold_in(arg_keys[10], 71), 0)
    target_lengths = draw_target_lengths(jax.random.fold_in(arg_keys[10], 71), 0)
    enc_pack = draw_enc_pack(jax.random.fold_in(arg_keys[10], 71), 0)
    dec_pack = draw_dec_pack(jax.random.fold_in(arg_keys[10], 71), 0)
    task_group = picks_of(arg_keys[8], N_DP * EX_GRP, GROUPS, 1, 1024).reshape((N_DP, EX_GRP, 1))
    dro_weights = with_ends(jax.random.randint(arg_keys[9], (GROUPS,), 1, 9), jax.random.fold_in(arg_keys[9], 1), 1, 8).astype(jnp.int32)
    return {"enc_keys": enc_keys, "enc_values": enc_values, "dec_queries": dec_queries, "cotangent": cotangent, "input_lengths": input_lengths, "target_lengths": target_lengths, "enc_pack": enc_pack, "dec_pack": dec_pack, "task_group": task_group, "dro_weights": dro_weights}


def owner_value(member, values):
    return jnp.sum(jnp.where(member, values[:, None], 0), axis=0).astype(values.dtype)


def pack_tables(lengths, pack_index, per_pack, slot_total, pack_total):
    ordinal = jnp.arange(lengths.shape[0], dtype=jnp.int32)
    same_pack = pack_index[:, None] == pack_index[None, :]
    earlier = ordinal[None, :] < ordinal[:, None]
    offsets = jnp.sum(jnp.where(same_pack & earlier, lengths[None, :], 0), axis=1).astype(jnp.int32)
    places = jnp.arange(slot_total, dtype=jnp.int32)
    inside = places[None, :] < lengths[:, None]
    starts = pack_index * per_pack + offsets
    gather_rows = (starts[:, None] + jnp.minimum(places[None, :], lengths[:, None] - 1)).astype(jnp.int32)
    tokens = jnp.arange(pack_total * per_pack, dtype=jnp.int32)
    token_pack = tokens // per_pack
    token_place = tokens % per_pack
    member = (pack_index[:, None] == token_pack[None, :]) & (offsets[:, None] <= token_place[None, :]) & (token_place[None, :] < (offsets + lengths)[:, None])
    owners = owner_value(member, ordinal)
    flat_slot = (owners * slot_total + token_place - owner_value(member, offsets)).astype(jnp.int32)
    return gather_rows, inside, member, flat_slot


def probabilities(query_split, key_split, key_inside):
    scores = jnp.einsum("qhd,khd->hqk", query_split, key_split)
    scores = jnp.where(key_inside[None, None, :], scores, -1e30)
    highest = jnp.max(scores, axis=-1, keepdims=True)
    powers = jnp.exp(scores - highest)
    return powers / jnp.sum(powers, axis=-1, keepdims=True)


def example_terms(query_rows, key_rows, value_rows, gradient, cotangent_rows, key_inside):
    query_slots = query_rows.shape[0]
    key_slots = key_rows.shape[0]
    query_split = query_rows.astype(jnp.float32).reshape(query_slots, HEADS, HEAD_DIM)
    key_split = key_rows.astype(jnp.float32).reshape(key_slots, HEADS, HEAD_DIM)
    value_split = value_rows.astype(jnp.float32).reshape(key_slots, HEADS, HEAD_DIM)
    gradient_split = gradient.astype(jnp.float32).reshape(query_slots, HEADS, HEAD_DIM)
    attention = probabilities(query_split, key_split, key_inside)
    attention_low = lax.optimization_barrier(attention.astype(jnp.bfloat16)).astype(jnp.float32)
    attended = jnp.einsum("hqk,khd->qhd", attention_low, value_split).astype(jnp.bfloat16)
    attended_split = lax.optimization_barrier(attended).astype(jnp.float32)
    token_loss = jnp.sum(attended_split.reshape(query_slots, -1) * cotangent_rows.astype(jnp.float32), axis=1)
    value_gradient = jnp.einsum("hqk,qhd->khd", attention_low, gradient_split).astype(jnp.bfloat16)
    attention_gradient = jnp.einsum("qhd,khd->hqk", gradient_split, value_split)
    row_drift = jnp.einsum("qhd,qhd->hq", gradient_split, attended_split)
    scores_gradient = (attention * (attention_gradient - row_drift[:, :, None])).astype(jnp.bfloat16)
    scores_gradient = lax.optimization_barrier(scores_gradient).astype(jnp.float32)
    query_gradient = jnp.einsum("hqk,khd->qhd", scores_gradient, key_split).astype(jnp.bfloat16)
    key_gradient = jnp.einsum("hqk,qhd->khd", scores_gradient, query_split).astype(jnp.bfloat16)
    return query_gradient.reshape(query_slots, -1), key_gradient.reshape(key_slots, -1), value_gradient.reshape(key_slots, -1), token_loss


def reference(enc_keys, enc_values, dec_queries, cotangent, input_lengths, target_lengths, enc_pack, dec_pack, task_group, dro_weights):
    group_index = jnp.arange(GROUPS, dtype=jnp.int32)
    task_ids = task_group[:, :, 0]
    counts = jnp.sum(jnp.where(task_ids[:, :, None] == group_index, target_lengths[:, :, None], 0), axis=(0, 1)).astype(jnp.float32)
    weights = dro_weights.astype(jnp.float32)
    scales = weights / jnp.sum(weights) * (DEC_TOKENS / counts)

    def one_group(entries):
        key_table, value_table, query_table, cotangent_rows, encoder_lengths, decoder_lengths, encoder_packs, decoder_packs, task_row = entries
        key_rows, key_inside, key_member, key_flat = pack_tables(encoder_lengths, encoder_packs, ENC_DEV, ENC_SLOT, N_PACK)
        query_rows, query_inside, query_member, query_flat = pack_tables(decoder_lengths, decoder_packs, DEC_DEV, DEC_SLOT, N_PACK)
        example_scale = jnp.sum(jnp.where(task_row[:, None] == group_index[None, :], scales[None, :], 0.0), axis=1)
        token_scale = owner_value(query_member, example_scale)
        token_group = owner_value(query_member, task_row)
        upstream = (cotangent_rows.astype(jnp.float32) * token_scale[:, None]).astype(jnp.bfloat16)

        def one_example(items):
            rows_query, rows_key, inside_key, inside_query = items
            gradient = jnp.where(inside_query[:, None], upstream[rows_query], jnp.zeros((), jnp.bfloat16))
            return example_terms(query_table[rows_query], key_table[rows_key], value_table[rows_key], gradient, cotangent_rows[rows_query], inside_key)

        query_padded, key_padded, value_padded, loss_padded = lax.map(one_example, (query_rows, key_rows, key_inside, query_inside))
        feature_width = query_table.shape[1]
        queries_result = query_padded.reshape(-1, feature_width)[query_flat]
        keys_result = key_padded.reshape(-1, feature_width)[key_flat]
        values_result = value_padded.reshape(-1, feature_width)[key_flat]
        token_loss = loss_padded.reshape(-1)[query_flat]
        partial_value = jnp.sum(jnp.where(token_group[None, :] == group_index[:, None], token_loss[None, :], 0.0), axis=1)
        return queries_result, keys_result, values_result, partial_value

    stacked = (enc_keys.reshape(N_DP, -1, D), enc_values.reshape(N_DP, -1, D), dec_queries.reshape(N_DP, -1, D), cotangent.reshape(N_DP, -1, D), input_lengths, target_lengths, enc_pack, dec_pack, task_ids)
    queries_gradient, keys_gradient, values_gradient, partials = lax.map(one_group, stacked)
    group_loss = jnp.sum(partials, axis=0) / counts
    return queries_gradient.reshape(-1, D), keys_gradient.reshape(-1, D), values_gradient.reshape(-1, D), group_loss
```

```python
import functools

import jax
import jax.numpy as jnp
from jax import lax
from jax.experimental import pallas as pl
from jax.experimental.pallas import tpu as pltpu
from jax.sharding import PartitionSpec as P

HEAD_DIM = 64
GROUPS = 16
NP = 32
SLOT = 15
PAIR = 2 * SLOT
TABLE = NP * 16
MESH = pl.DeviceIdType.MESH


def kernel(
    qstart, eslot, first, mine, scale,
    k_hbm, v_hbm, q_hbm, c_hbm,
    dq_out, dk_out, dv_out, loss_out,
    kv, vv, qt, ct, sq, sc, qin, cin, sd, bq, dp, dks, dvs,
    lsem, s1q, r1q, s1c, r1c, s2q, r2q, s2c, r2c, s3, r3, s4, r4, ksem, vsem,
):
    me = lax.axis_index("pack")

    def peer(k):
        return lax.rem(me + k, NP)

    def back(k):
        return lax.rem(me - k + NP, NP)

    def cols(i):
        return pl.ds(pl.multiple_of(i * 128, 128), 128)

    load_k = pltpu.make_async_copy(k_hbm, kv, lsem.at[0])
    load_v = pltpu.make_async_copy(v_hbm, vv, lsem.at[1])

    barrier = pltpu.get_barrier_semaphore()

    def greet(k, carry):
        pl.semaphore_signal(barrier, inc=1, device_id={"pack": peer(k)}, device_id_type=MESH)
        return carry

    lax.fori_loop(1, NP, greet, 0)
    pl.semaphore_wait(barrier, NP - 1)

    def spread(src, dst, send, recv):
        def make(k):
            return pltpu.make_async_remote_copy(
                src_ref=src.at[:, :, cols(peer(k))],
                dst_ref=dst.at[pl.ds(me * 16, 16)],
                send_sem=send.at[k],
                recv_sem=recv.at[k],
                device_id={"pack": peer(k)},
                device_id_type=MESH,
            )
        return make

    def run(count_from, body):
        def step(k, carry):
            body(k)
            return carry
        lax.fori_loop(count_from, NP, step, 0)

    q1 = spread(q_hbm, qt, s1q, r1q)
    c1 = spread(c_hbm, ct, s1c, r1c)
    own_q = pltpu.make_async_copy(q_hbm.at[:, :, cols(me)], qt.at[pl.ds(me * 16, 16)], lsem.at[2])
    own_c = pltpu.make_async_copy(c_hbm.at[:, :, cols(me)], ct.at[pl.ds(me * 16, 16)], lsem.at[3])
    run(1, lambda k: q1(k).start())
    own_q.start()
    run(1, lambda k: c1(k).start())
    own_c.start()
    load_k.start()
    load_v.start()
    qt[pl.ds(TABLE, 16)] = jnp.zeros((16, 8, 128), jnp.bfloat16)
    ct[pl.ds(TABLE, 16)] = jnp.zeros((16, 8, 128), jnp.bfloat16)

    def deal(table, send_buf, into, send, recv):
        def make(k):
            return pltpu.make_async_remote_copy(
                src_ref=send_buf.at[k],
                dst_ref=into.at[k],
                send_sem=send.at[k],
                recv_sem=recv.at[k],
                device_id={"pack": peer(k)},
                device_id_type=MESH,
            )

        def fill(k, dst):
            p = peer(k)
            for a in range(2):
                start = qstart[2 * p + a]
                dst[k, pl.ds(a * SLOT, SLOT)] = table[pl.ds(start, SLOT)]

        return make, fill

    q2, fill_q = deal(qt, sq, qin, s2q, r2q)
    c2, fill_c = deal(ct, sc, cin, s2c, r2c)

    def arrived_1(make, i):
        make(i).wait_recv()

    run(1, lambda k: q1(k).wait_recv())
    own_q.wait()

    def send_q(k):
        fill_q(k, sq)
        q2(k).start()

    run(1, send_q)
    fill_q(0, qin)

    run(1, lambda k: c1(k).wait_recv())
    own_c.wait()

    def send_c(k):
        fill_c(k, sc)
        c2(k).start()

    run(1, send_c)
    fill_c(0, cin)
    load_k.wait()
    load_v.wait()

    len0 = mine[0]
    len1 = mine[1]
    keys0 = mine[2]
    scale0 = scale[0]
    scale1 = scale[1]
    place_c = lax.broadcasted_iota(jnp.int32, (256, 1), 0)
    place_r = lax.broadcasted_iota(jnp.int32, (1, 256), 1)

    def valid_of(place):
        return jnp.where(place < 120, place < len0, place - 120 < len1)

    scale_c = jnp.where(place_c < 120, scale0, scale1)
    scale_r = jnp.where(place_r < 120, scale0, scale1)
    live_c = jnp.where(place_c < 120, jnp.where(place_c < len0, 1.0, 0.0), jnp.where(place_c - 120 < len1, 1.0, 0.0))
    live_r = jnp.where(place_r < 120, jnp.where(place_r < len0, 1.0, 0.0), jnp.where(place_r - 120 < len1, 1.0, 0.0))
    live_c2 = jnp.broadcast_to(live_c, (256, 128)) > 0.5
    live_r2 = jnp.broadcast_to(live_r, (128, 256)) > 0.5
    lane = lax.broadcasted_iota(jnp.int32, (256, 128), 1)
    key_place = lax.broadcasted_iota(jnp.int32, (256, 256), 0)
    query_place = lax.broadcasted_iota(jnp.int32, (256, 256), 1)
    bias = jnp.where(
        jnp.where(query_place < 120, key_place, keys0) < jnp.where(query_place < 120, keys0, key_place + 1),
        0.0, -1e30,
    ).astype(jnp.float32)
    nt = (((1,), (1,)), ((), ()))
    nn = (((1,), (0,)), ((), ()))

    def dot(a, b, dims):
        return lax.dot_general(a, b, dims, preferred_element_type=jnp.float32)

    def flat(ref, k):
        block = ref[k].astype(jnp.float32).reshape(240, 128)
        return jnp.concatenate([block, jnp.zeros((16, 128), jnp.float32)], axis=0)

    def d3(k):
        return pltpu.make_async_remote_copy(
            src_ref=sd.at[k],
            dst_ref=bq.at[pl.ds(me * PAIR, PAIR)],
            send_sem=s3.at[k],
            recv_sem=r3.at[k],
            device_id={"pack": back(k)},
            device_id_type=MESH,
        )

    def out_k(k):
        return pltpu.make_async_copy(dks.at[k], dk_out.at[:, cols(back(k))], ksem.at[k])

    def out_v(k):
        return pltpu.make_async_copy(dvs.at[k], dv_out.at[:, cols(back(k))], vsem.at[k])

    def compute(k, loss):
        i = back(k)
        q = flat(qin, k)
        c = flat(cin, k)
        kb = kv[:, cols(i)]
        vb = vv[:, cols(i)]
        k_t = kb.T
        v_t = vb.T
        c_t = c.T
        u = jnp.where(live_c2, (c * scale_c).astype(jnp.bfloat16).astype(jnp.float32), 0.0)
        u_t = jnp.where(live_r2, (c_t * scale_r).astype(jnp.bfloat16).astype(jnp.float32), 0.0)
        dk = jnp.zeros((256, 128), jnp.float32)
        dv = jnp.zeros((256, 128), jnp.float32)
        dq_parts = []
        for h in range(2):
            own = (lane < 64) if h == 0 else (lane >= 64)
            q_h = jnp.where(own, q, 0.0).astype(jnp.bfloat16)
            u_h = jnp.where(own, u, 0.0).astype(jnp.bfloat16)
            scores = dot(kb, q_h, nt) + bias
            highest = jnp.max(scores, axis=0, keepdims=True)
            powers = jnp.exp(scores - highest)
            attention = powers * (1.0 / jnp.sum(powers, axis=0, keepdims=True))
            low = attention.astype(jnp.bfloat16)
            attended = dot(v_t[h * 64:(h + 1) * 64], low, nn).astype(jnp.bfloat16).astype(jnp.float32)
            loss = loss + jnp.sum(attended * c_t[h * 64:(h + 1) * 64], axis=0, keepdims=True)
            drift = jnp.sum(attended * u_t[h * 64:(h + 1) * 64], axis=0, keepdims=True)
            dv = dv + dot(low, u_h, nn)
            grad = dot(vb, u_h, nt)
            ds = (attention * (grad - drift)).astype(jnp.bfloat16)
            dq_parts.append(dot(k_t[h * 64:(h + 1) * 64], ds, nn))
            dk = dk + dot(ds, q_h, nn)
        dq = jnp.concatenate(dq_parts, axis=0).T
        dks[k] = dk.astype(jnp.bfloat16)
        dvs[k] = dv.astype(jnp.bfloat16)
        sd_block = dq[:240].reshape(PAIR, 8, 128).astype(jnp.bfloat16)
        return sd_block, loss

    block, loss = compute(0, jnp.zeros((1, 256), jnp.float32))
    bq[pl.ds(me * PAIR, PAIR)] = block
    out_k(0).start()
    out_v(0).start()

    def pair_step(k, loss):
        q2(k).wait_recv()
        c2(k).wait_recv()
        block, loss = compute(k, loss)
        sd[k] = block
        d3(k).start()
        out_k(k).start()
        out_v(k).start()
        return loss

    loss = lax.fori_loop(1, NP, pair_step, loss)
    loss_out[...] = jnp.where(live_r > 0.5, loss, 0.0)

    run(1, lambda k: d3(k).wait_recv())

    def d4(k):
        return pltpu.make_async_remote_copy(
            src_ref=dp.at[k],
            dst_ref=dq_out.at[:, :, cols(me)],
            send_sem=s4.at[k],
            recv_sem=r4.at[k],
            device_id={"pack": peer(k)},
            device_id_type=MESH,
        )

    own_d = pltpu.make_async_copy(dp.at[0], dq_out.at[:, :, cols(me)], lsem.at[4])

    def fill_d(k):
        d = peer(k)
        near = eslot[2 * d] * SLOT
        count = first[d]
        far = eslot[2 * d + 1] * SLOT - count
        for b in range(16):
            dp[k, b] = bq[jnp.where(b < count, near, far) + b]

    def send_d(k):
        fill_d(k)
        d4(k).start()

    run(1, send_d)
    fill_d(0)
    own_d.start()

    def drain(k):
        q1(k).wait_send()
        c1(k).wait_send()
        q2(k).wait_send()
        c2(k).wait_send()
        d3(k).wait_send()
        out_k(k).wait()
        out_v(k).wait()
        d4(k).wait_send()
        d4(k).wait_recv()

    run(1, drain)
    out_k(0).wait()
    out_v(0).wait()
    own_d.wait()


def local(
    enc_keys, enc_values, dec_queries, cotangent,
    input_lengths, target_lengths, enc_pack, dec_pack, task_group, dro_weights,
):
    me = lax.axis_index("pack")
    lens_e, lens_d = input_lengths[0], target_lengths[0]
    ep, dpk, task = enc_pack[0], dec_pack[0], task_group[0, :, 0]
    ordinal = jnp.arange(64, dtype=jnp.int32)
    earlier = ordinal[None, :] < ordinal[:, None]
    same_e = earlier & (ep[:, None] == ep[None, :])
    same_d = earlier & (dpk[:, None] == dpk[None, :])
    slot_e = ep * 2 + jnp.sum(same_e, axis=1).astype(jnp.int32)
    slot_d = dpk * 2 + jnp.sum(same_d, axis=1).astype(jnp.int32)
    start_d = dpk * 16 + jnp.sum(jnp.where(same_d, lens_d[None, :], 0), axis=1) // 8
    at_e = slot_e[None, :] == ordinal[:, None]
    at_d = slot_d[None, :] == ordinal[:, None]

    def pick(at, values):
        return jnp.sum(jnp.where(at, values[None, :], 0), axis=1)

    qstart = pick(at_e, start_d)
    qlen = pick(at_e, lens_d)
    klen = pick(at_e, lens_e)
    qgroup = pick(at_e, task)
    eslot = pick(at_d, slot_e)
    dlen = pick(at_d, lens_d)
    first = dlen.reshape(NP, 2)[:, 0] // 8

    group_index = jnp.arange(GROUPS, dtype=jnp.int32)
    part = jnp.sum(jnp.where(task[:, None] == group_index[None, :], lens_d[:, None], 0), axis=0)
    counts = lax.psum(part.astype(jnp.float32), "dp")
    weights = dro_weights.astype(jnp.float32)
    total = 128 * NP * lax.axis_size("dp")
    scales = weights / jnp.sum(weights) * (total / counts)

    own_len = lax.dynamic_slice_in_dim(qlen, 2 * me, 2)
    own_keys = lax.dynamic_slice_in_dim(klen, 2 * me, 2)
    own_group = lax.dynamic_slice_in_dim(qgroup, 2 * me, 2)
    mine = jnp.concatenate([own_len, own_keys])
    own_match = own_group[:, None] == group_index[None, :]
    own_scale = jnp.sum(jnp.where(own_match, scales[None, :], 0.0), axis=1)

    bf = jnp.bfloat16
    smem = pl.BlockSpec(memory_space=pltpu.SMEM)
    hbm = pl.BlockSpec(memory_space=pl.ANY)
    dma = pltpu.SemaphoreType.DMA
    dq, dk, dv, loss = pl.pallas_call(
        kernel,
        out_shape=(
            jax.ShapeDtypeStruct((16, 8, 4096), bf),
            jax.ShapeDtypeStruct((256, 4096), bf),
            jax.ShapeDtypeStruct((256, 4096), bf),
            jax.ShapeDtypeStruct((1, 256), jnp.float32),
        ),
        in_specs=[smem] * 5 + [hbm] * 4,
        out_specs=(hbm, hbm, hbm, pl.BlockSpec(memory_space=pltpu.VMEM)),
        scratch_shapes=[
            pltpu.VMEM((256, 4096), bf),
            pltpu.VMEM((256, 4096), bf),
            pltpu.VMEM((TABLE + 16, 8, 128), bf),
            pltpu.VMEM((TABLE + 16, 8, 128), bf),
            pltpu.VMEM((NP, PAIR, 8, 128), bf),
            pltpu.VMEM((NP, PAIR, 8, 128), bf),
            pltpu.VMEM((NP, PAIR, 8, 128), bf),
            pltpu.VMEM((NP, PAIR, 8, 128), bf),
            pltpu.VMEM((NP, PAIR, 8, 128), bf),
            pltpu.VMEM((NP * PAIR, 8, 128), bf),
            pltpu.VMEM((NP, 16, 8, 128), bf),
            pltpu.VMEM((NP, 256, 128), bf),
            pltpu.VMEM((NP, 256, 128), bf),
            dma((8,)),
        ] + [dma((NP,))] * 14,
        compiler_params=pltpu.CompilerParams(
            collective_id=0, has_side_effects=True, vmem_limit_bytes=56 * 1024 * 1024
        ),
        cost_estimate=pl.CostEstimate(flops=3_000_000_000, bytes_accessed=11_000_000, transcendentals=4_000_000),
    )(
        qstart, eslot, first, mine, own_scale,
        enc_keys, enc_values,
        dec_queries.reshape(16, 8, 4096), cotangent.reshape(16, 8, 4096),
    )
    token_loss = loss[0]
    example_loss = jnp.stack([jnp.sum(token_loss[:120]), jnp.sum(token_loss[120:])])
    loss_part = jnp.sum(jnp.where(own_match, example_loss[:, None], 0.0), axis=0)
    group_loss = lax.psum(loss_part, ("dp", "pack")) / counts
    return dq.reshape(128, 4096), dk, dv, group_loss


def solution(mesh):
    rows = P(("dp", "pack"), None)
    small = P("dp", None)
    return jax.shard_map(
        local,
        mesh=mesh,
        in_specs=(rows, rows, rows, rows, small, small, small, small, P("dp", None, None), P()),
        out_specs=(rows, rows, rows, P()),
        check_vma=False,
    )
```

```python
import functools

import jax
import jax.numpy as jnp
from jax import lax
from jax.experimental import pallas as pl
from jax.experimental.pallas import tpu as pltpu
from jax.sharding import PartitionSpec as P

HEAD_DIM = 64
GROUPS = 16
NP = 32
SLOT = 15
PAIR = 2 * SLOT
TABLE = NP * 16
MESH = pl.DeviceIdType.MESH


def kernel(
    lens_e_ref, lens_d_ref, ep_ref, dpk_ref, task_ref, dro_ref,
    k_hbm, v_hbm, q_hbm, c_hbm,
    dq_out, dk_out, dv_out, loss_out,
    kv, vv, qt, ct, sq, sc, qin, cin, sd, bq, dp, dks, dvs,
    tab_v, tab, cnt, lpart, lz,
    lsem, s1q, r1q, s1c, r1c, s2q, r2q, s2c, r2c, s3, r3, s4, r4, ksem, vsem, sl, rl, szc, rzc, szl, rzl,
):
    me = lax.axis_index("pack")
    z = lax.axis_index("dp")
    nz = lax.axis_size("dp")
    x, y, core = me // 8, lax.rem(me // 2, 4), lax.rem(me, 2)

    def other(k, source):
        j = k // 2
        dx, dy = lax.rem(j, 4), lax.rem(j // 4 + j, 4)
        far = lax.rem(core + k, 2)
        sign = (2 * far - 1) if source else (1 - 2 * core)
        return lax.rem(x + sign * dx + 4, 4) * 8 + lax.rem(y + sign * dy + 4, 4) * 2 + far

    def peer(k):
        return other(k, False)

    def back(k):
        return other(k, True)

    def cols(i):
        return pl.ds(pl.multiple_of(i * 128, 128), 128)

    def zpeer(k):
        return lax.rem(z + k, nz)

    load_k = pltpu.make_async_copy(k_hbm, kv, lsem.at[0])
    load_v = pltpu.make_async_copy(v_hbm, vv, lsem.at[1])

    barrier = pltpu.get_barrier_semaphore()

    def greet(k, carry):
        pl.semaphore_signal(barrier, inc=1, device_id={"pack": peer(k)}, device_id_type=MESH)
        return carry

    def greet_z(k, carry):
        pl.semaphore_signal(barrier, inc=1, device_id={"dp": zpeer(k)}, device_id_type=MESH)
        return carry

    lax.fori_loop(1, NP, greet, 0)
    lax.fori_loop(1, nz, greet_z, 0)
    pl.semaphore_wait(barrier, NP + nz - 2)

    def spread(src, dst, send, recv):
        def make(k):
            return pltpu.make_async_remote_copy(
                src_ref=src.at[:, :, cols(peer(k))],
                dst_ref=dst.at[pl.ds(me * 16, 16)],
                send_sem=send.at[k],
                recv_sem=recv.at[k],
                device_id={"pack": peer(k)},
                device_id_type=MESH,
            )
        return make

    def run(count_from, body):
        def step(k, carry):
            body(k)
            return carry
        lax.fori_loop(count_from, NP, step, 0)

    q1 = spread(q_hbm, qt, s1q, r1q)
    c1 = spread(c_hbm, ct, s1c, r1c)
    own_q = pltpu.make_async_copy(q_hbm.at[:, :, cols(me)], qt.at[pl.ds(me * 16, 16)], lsem.at[2])
    own_c = pltpu.make_async_copy(c_hbm.at[:, :, cols(me)], ct.at[pl.ds(me * 16, 16)], lsem.at[3])
    run(1, lambda k: q1(k).start())
    own_q.start()
    run(1, lambda k: c1(k).start())
    own_c.start()
    load_k.start()
    load_v.start()
    qt[pl.ds(TABLE, 16)] = jnp.zeros((16, 8, 128), jnp.bfloat16)
    ct[pl.ds(TABLE, 16)] = jnp.zeros((16, 8, 128), jnp.bfloat16)
    bq[pl.ds(NP * PAIR, 16)] = jnp.zeros((16, 8, 128), jnp.bfloat16)

    f32 = jnp.float32
    i32 = jnp.int32
    lens_e_r = lens_e_ref[...]
    lens_d_r = lens_d_ref[...]
    ep_r = ep_ref[...]
    dpk_r = dpk_ref[...]
    at_row = lax.broadcasted_iota(i32, (64, 64), 0)
    at_col = lax.broadcasted_iota(i32, (64, 64), 1)

    def column(row):
        return jnp.sum(jnp.where(at_row == at_col, row, 0), axis=1, keepdims=True)

    lens_d_c = column(lens_d_r)
    group = lax.broadcasted_iota(i32, (64, 128), 1)
    part = jnp.sum(jnp.where(column(task_ref[...]) == group, lens_d_c, 0), axis=0, keepdims=True)
    cnt[z] = jnp.broadcast_to(part.astype(f32), (8, 128))

    def count_copy(k):
        return pltpu.make_async_remote_copy(
            src_ref=cnt.at[z],
            dst_ref=cnt.at[z],
            send_sem=szc.at[k],
            recv_sem=rzc.at[k],
            device_id={"dp": zpeer(k)},
            device_id_type=MESH,
        )

    def count_arrival(k):
        source = lax.rem(z - k + nz, nz)
        return pltpu.make_async_remote_copy(
            src_ref=cnt.at[source],
            dst_ref=cnt.at[source],
            send_sem=szc.at[k],
            recv_sem=rzc.at[k],
            device_id={"dp": source},
            device_id_type=MESH,
        )

    def run_z(body):
        def step(k, carry):
            body(k)
            return carry
        lax.fori_loop(1, nz, step, 0)

    run_z(lambda k: count_copy(k).start())

    ahead_e = jnp.where(column(ep_r) == ep_r, jnp.where(at_row < at_col, 1, 0), 0)
    ahead_d = jnp.where(column(dpk_r) == dpk_r, jnp.where(at_row < at_col, 1, 0), 0)
    slot_e_r = 2 * ep_r + jnp.sum(ahead_e, axis=0, keepdims=True)
    slot_d_r = 2 * dpk_r + jnp.sum(ahead_d, axis=0, keepdims=True)
    start_r = 16 * dpk_r + jnp.sum(ahead_d * lens_d_c, axis=0, keepdims=True) // 8

    def pick(slot_r, values_r):
        return jnp.sum(jnp.where(slot_r == at_row, values_r, 0), axis=1, keepdims=True)

    columns = (
        pick(slot_e_r, start_r), pick(slot_e_r, lens_d_r), pick(slot_e_r, lens_e_r), pick(slot_e_r, task_ref[...]),
        pick(slot_d_r, slot_e_r), pick(slot_d_r, lens_d_r),
    )
    wide = jnp.zeros((64, 128), i32)
    for at, values in enumerate(columns):
        wide = jnp.where(group == at, values, wide)
    wide = jnp.concatenate([wide, jnp.zeros((64, 128), i32)], axis=0)
    tab_v[...] = wide.T[:8]
    table_copy = pltpu.make_async_copy(tab_v, tab, lsem.at[5])
    table_copy.start()
    table_copy.wait()

    def deal(table, send_buf, into, send, recv):
        def make(k):
            return pltpu.make_async_remote_copy(
                src_ref=send_buf.at[k],
                dst_ref=into.at[k],
                send_sem=send.at[k],
                recv_sem=recv.at[k],
                device_id={"pack": peer(k)},
                device_id_type=MESH,
            )

        def fill(k, dst):
            p = peer(k)
            for a in range(2):
                start = jnp.clip(tab[0, 2 * p + a], 0, TABLE)
                dst[k, pl.ds(a * SLOT, SLOT)] = table[pl.ds(start, SLOT)]

        return make, fill

    q2, fill_q = deal(qt, sq, qin, s2q, r2q)
    c2, fill_c = deal(ct, sc, cin, s2c, r2c)

    def arrived_1(make, i):
        make(i).wait_recv()

    run(1, lambda k: q1(k).wait_recv())
    own_q.wait()

    def send_q(k):
        fill_q(k, sq)
        q2(k).start()

    run(1, send_q)
    fill_q(0, qin)

    run(1, lambda k: c1(k).wait_recv())
    own_c.wait()

    def send_c(k):
        fill_c(k, sc)
        c2(k).start()

    run(1, send_c)
    fill_c(0, cin)
    load_k.wait()
    load_v.wait()

    len0 = tab[1, 2 * me]
    len1 = tab[1, 2 * me + 1]
    keys0 = tab[2, 2 * me]
    run_z(lambda k: count_arrival(k).wait_recv())
    counts = cnt[0][:1]
    for at in range(1, nz):
        counts = counts + cnt[at][:1]
    lane_r = lax.broadcasted_iota(jnp.int32, (1, 128), 1)
    weights = jnp.concatenate([dro_ref[...].astype(f32), jnp.zeros((1, 128 - GROUPS), f32)], axis=1)
    scales = weights / jnp.sum(weights, axis=1, keepdims=True) * (128.0 * NP * nz / counts)
    own0 = lane_r == tab[3, 2 * me]
    own1 = lane_r == tab[3, 2 * me + 1]
    scale0 = jnp.sum(jnp.where(own0, scales, 0.0), axis=1, keepdims=True)
    scale1 = jnp.sum(jnp.where(own1, scales, 0.0), axis=1, keepdims=True)
    place_c = lax.broadcasted_iota(jnp.int32, (256, 1), 0)
    place_r = lax.broadcasted_iota(jnp.int32, (1, 256), 1)

    def valid_of(place):
        return jnp.where(place < 120, place < len0, place - 120 < len1)

    scale_c = jnp.where(place_c < 120, scale0, scale1)
    scale_r = jnp.where(place_r < 120, scale0, scale1)
    live_c = jnp.where(place_c < 120, jnp.where(place_c < len0, 1.0, 0.0), jnp.where(place_c - 120 < len1, 1.0, 0.0))
    live_r = jnp.where(place_r < 120, jnp.where(place_r < len0, 1.0, 0.0), jnp.where(place_r - 120 < len1, 1.0, 0.0))
    live_c2 = jnp.broadcast_to(live_c, (256, 128)) > 0.5
    live_r2 = jnp.broadcast_to(live_r, (128, 256)) > 0.5
    lane = lax.broadcasted_iota(jnp.int32, (256, 128), 1)
    key_place = lax.broadcasted_iota(jnp.int32, (256, 256), 0)
    query_place = lax.broadcasted_iota(jnp.int32, (256, 256), 1)
    bias = jnp.where(
        jnp.where(query_place < 120, key_place, keys0) < jnp.where(query_place < 120, keys0, key_place + 1),
        0.0, -1e30,
    ).astype(jnp.float32)
    nt = (((1,), (1,)), ((), ()))
    nn = (((1,), (0,)), ((), ()))

    def dot(a, b, dims):
        return lax.dot_general(a, b, dims, preferred_element_type=jnp.float32)

    def flat(ref, k):
        block = ref[k].astype(jnp.float32).reshape(240, 128)
        return jnp.concatenate([block, jnp.zeros((16, 128), jnp.float32)], axis=0)

    def d3(k):
        return pltpu.make_async_remote_copy(
            src_ref=sd.at[k],
            dst_ref=bq.at[pl.ds(me * PAIR, PAIR)],
            send_sem=s3.at[k],
            recv_sem=r3.at[k],
            device_id={"pack": back(k)},
            device_id_type=MESH,
        )

    def out_k(k):
        return pltpu.make_async_copy(dks.at[k], dk_out.at[:, cols(back(k))], ksem.at[k])

    def out_v(k):
        return pltpu.make_async_copy(dvs.at[k], dv_out.at[:, cols(back(k))], vsem.at[k])

    def compute(k, loss):
        i = back(k)
        q = flat(qin, k)
        c = flat(cin, k)
        kb = kv[:, cols(i)]
        vb = vv[:, cols(i)]
        k_t = kb.T
        v_t = vb.T
        c_t = c.T
        u = jnp.where(live_c2, (c * scale_c).astype(jnp.bfloat16).astype(jnp.float32), 0.0)
        u_t = jnp.where(live_r2, (c_t * scale_r).astype(jnp.bfloat16).astype(jnp.float32), 0.0)
        dk = jnp.zeros((256, 128), jnp.float32)
        dv = jnp.zeros((256, 128), jnp.float32)
        dq_parts = []
        for h in range(2):
            own = (lane < 64) if h == 0 else (lane >= 64)
            q_h = jnp.where(own, q, 0.0).astype(jnp.bfloat16)
            u_h = jnp.where(own, u, 0.0).astype(jnp.bfloat16)
            scores = dot(kb, q_h, nt) + bias
            highest = jnp.max(scores, axis=0, keepdims=True)
            powers = jnp.exp(scores - highest)
            attention = powers * (1.0 / jnp.sum(powers, axis=0, keepdims=True))
            low = attention.astype(jnp.bfloat16)
            attended = dot(v_t[h * 64:(h + 1) * 64], low, nn).astype(jnp.bfloat16).astype(jnp.float32)
            loss = loss + jnp.sum(attended * c_t[h * 64:(h + 1) * 64], axis=0, keepdims=True)
            drift = jnp.sum(attended * u_t[h * 64:(h + 1) * 64], axis=0, keepdims=True)
            dv = dv + dot(low, u_h, nn)
            grad = dot(vb, u_h, nt)
            ds = (attention * (grad - drift)).astype(jnp.bfloat16)
            dq_parts.append(dot(k_t[h * 64:(h + 1) * 64], ds, nn))
            dk = dk + dot(ds, q_h, nn)
        dq = jnp.concatenate(dq_parts, axis=0).T
        dks[k] = dk.astype(jnp.bfloat16)
        dvs[k] = dv.astype(jnp.bfloat16)
        sd_block = dq[:240].reshape(PAIR, 8, 128).astype(jnp.bfloat16)
        return sd_block, loss

    block, loss = compute(0, jnp.zeros((1, 256), jnp.float32))
    bq[pl.ds(me * PAIR, PAIR)] = block
    out_k(0).start()
    out_v(0).start()

    def pair_step(k, loss):
        q2(k).wait_recv()
        c2(k).wait_recv()
        block, loss = compute(k, loss)
        sd[k] = block
        d3(k).start()
        out_k(k).start()
        out_v(k).start()
        return loss

    loss = lax.fori_loop(1, NP, pair_step, loss)
    loss = jnp.where(live_r > 0.5, loss, 0.0)
    loss0 = jnp.sum(jnp.where(place_r < 120, loss, 0.0), axis=1, keepdims=True)
    loss1 = jnp.sum(jnp.where(place_r < 120, 0.0, loss), axis=1, keepdims=True)
    own_loss = jnp.where(own0, loss0, 0.0) + jnp.where(own1, loss1, 0.0)
    lpart[me] = jnp.broadcast_to(own_loss, (8, 128))

    def loss_copy(k):
        return pltpu.make_async_remote_copy(
            src_ref=lpart.at[me],
            dst_ref=lpart.at[me],
            send_sem=sl.at[k],
            recv_sem=rl.at[k],
            device_id={"pack": peer(k)},
            device_id_type=MESH,
        )

    def loss_arrival(k):
        return pltpu.make_async_remote_copy(
            src_ref=lpart.at[back(k)],
            dst_ref=lpart.at[back(k)],
            send_sem=sl.at[k],
            recv_sem=rl.at[k],
            device_id={"pack": back(k)},
            device_id_type=MESH,
        )

    run(1, lambda k: loss_copy(k).start())

    run(1, lambda k: d3(k).wait_recv())

    def d4(k):
        return pltpu.make_async_remote_copy(
            src_ref=dp.at[k],
            dst_ref=dq_out.at[:, :, cols(me)],
            send_sem=s4.at[k],
            recv_sem=r4.at[k],
            device_id={"pack": peer(k)},
            device_id_type=MESH,
        )

    own_d = pltpu.make_async_copy(dp.at[0], dq_out.at[:, :, cols(me)], lsem.at[4])

    def fill_d(k):
        d = peer(k)
        near = tab[4, 2 * d] * SLOT
        count = tab[5, 2 * d] // 8
        far = tab[4, 2 * d + 1] * SLOT - count
        for b in range(16):
            dp[k, b] = bq[jnp.clip(jnp.where(b < count, near, far) + b, 0, NP * PAIR - 1)]

    def send_d(k):
        fill_d(k)
        d4(k).start()

    run(1, send_d)
    fill_d(0)
    own_d.start()

    run(1, lambda k: loss_arrival(k).wait_recv())
    lz[z] = jnp.sum(lpart[...], axis=0)

    def zloss_copy(k):
        return pltpu.make_async_remote_copy(
            src_ref=lz.at[z],
            dst_ref=lz.at[z],
            send_sem=szl.at[k],
            recv_sem=rzl.at[k],
            device_id={"dp": zpeer(k)},
            device_id_type=MESH,
        )

    def zloss_arrival(k):
        source = lax.rem(z - k + nz, nz)
        return pltpu.make_async_remote_copy(
            src_ref=lz.at[source],
            dst_ref=lz.at[source],
            send_sem=szl.at[k],
            recv_sem=rzl.at[k],
            device_id={"dp": source},
            device_id_type=MESH,
        )

    run_z(lambda k: zloss_copy(k).start())
    run_z(lambda k: zloss_arrival(k).wait_recv())
    total = jnp.sum(lz[...], axis=0)[:1] / counts
    loss_out[...] = total[:, :GROUPS]

    def drain_z(k):
        count_copy(k).wait_send()
        zloss_copy(k).wait_send()

    run_z(drain_z)

    def drain(k):
        loss_copy(k).wait_send()
        q1(k).wait_send()
        c1(k).wait_send()
        q2(k).wait_send()
        c2(k).wait_send()
        d3(k).wait_send()
        out_k(k).wait()
        out_v(k).wait()
        d4(k).wait_send()
        d4(k).wait_recv()

    run(1, drain)
    out_k(0).wait()
    out_v(0).wait()
    own_d.wait()


def local(
    enc_keys, enc_values, dec_queries, cotangent,
    input_lengths, target_lengths, enc_pack, dec_pack, task_group, dro_weights,
):
    bf = jnp.bfloat16
    vmem = pl.BlockSpec(memory_space=pltpu.VMEM)
    hbm = pl.BlockSpec(memory_space=pl.ANY)
    nz = lax.axis_size("dp")
    dma = pltpu.SemaphoreType.DMA
    dq, dk, dv, loss = pl.pallas_call(
        kernel,
        out_shape=(
            jax.ShapeDtypeStruct((16, 8, 4096), bf),
            jax.ShapeDtypeStruct((256, 4096), bf),
            jax.ShapeDtypeStruct((256, 4096), bf),
            jax.ShapeDtypeStruct((1, GROUPS), jnp.float32),
        ),
        in_specs=[vmem] * 6 + [hbm] * 4,
        out_specs=(hbm, hbm, hbm, vmem),
        scratch_shapes=[
            pltpu.VMEM((256, 4096), bf),
            pltpu.VMEM((256, 4096), bf),
            pltpu.VMEM((TABLE + 16, 8, 128), bf),
            pltpu.VMEM((TABLE + 16, 8, 128), bf),
            pltpu.VMEM((NP, PAIR, 8, 128), bf),
            pltpu.VMEM((NP, PAIR, 8, 128), bf),
            pltpu.VMEM((NP, PAIR, 8, 128), bf),
            pltpu.VMEM((NP, PAIR, 8, 128), bf),
            pltpu.VMEM((NP, PAIR, 8, 128), bf),
            pltpu.VMEM((NP * PAIR + 16, 8, 128), bf),
            pltpu.VMEM((NP, 16, 8, 128), bf),
            pltpu.VMEM((NP, 256, 128), bf),
            pltpu.VMEM((NP, 256, 128), bf),
            pltpu.VMEM((8, 128), jnp.int32),
            pltpu.SMEM((8, 128), jnp.int32),
            pltpu.VMEM((nz, 8, 128), jnp.float32),
            pltpu.VMEM((NP, 8, 128), jnp.float32),
            pltpu.VMEM((nz, 8, 128), jnp.float32),
            dma((8,)),
        ] + [dma((NP,))] * 16 + [dma((nz,))] * 4,
        compiler_params=pltpu.CompilerParams(
            collective_id=0, has_side_effects=True, vmem_limit_bytes=56 * 1024 * 1024
        ),
        cost_estimate=pl.CostEstimate(flops=3_000_000_000, bytes_accessed=11_000_000, transcendentals=4_000_000),
    )(
        input_lengths, target_lengths, enc_pack, dec_pack, task_group.reshape(1, 64), dro_weights.reshape(1, GROUPS),
        enc_keys, enc_values,
        dec_queries.reshape(16, 8, 4096), cotangent.reshape(16, 8, 4096),
    )
    return dq.reshape(128, 4096), dk, dv, loss.reshape(GROUPS)


def solution(mesh):
    rows = P(("dp", "pack"), None)
    small = P("dp", None)
    return jax.shard_map(
        local,
        mesh=mesh,
        in_specs=(rows, rows, rows, rows, small, small, small, small, P("dp", None, None), P()),
        out_specs=(rows, rows, rows, P()),
        check_vma=False,
    )
```

```python
import functools

import jax
import jax.numpy as jnp
from jax import lax
from jax.experimental import pallas as pl
from jax.experimental.pallas import tpu as pltpu
from jax.sharding import PartitionSpec as P

HEAD_DIM = 64
GROUPS = 16
NP = 32
SLOT = 15
PAIR = 2 * SLOT
TABLE = NP * 16
MESH = pl.DeviceIdType.MESH


def kernel(
    lens_e_ref, lens_d_ref, ep_ref, dpk_ref, task_ref, dro_ref,
    k_hbm, v_hbm, q_hbm, c_hbm,
    dq_out, dk_out, dv_out, loss_out,
    kv, vv, qt, ct, sq, sc, qin, cin, sd, bq, dp,
    tab_v, tab, cnt, lpart, lz, ctot, ltot,
    lsem, one, r2q, r2c,
):
    s1q, r1q, s1c, r1c, s2q, s2c, s3, r3, s4, r4, sl, rl, szc, rzc, szl, rzl, szt, rzt, szm, rzm = (
        one.at[at] for at in range(20)
    )
    me = lax.axis_index("pack")
    z = lax.axis_index("dp")
    nz = lax.axis_size("dp")
    x, y, core = me // 8, lax.rem(me // 2, 4), lax.rem(me, 2)

    def other(k, source):
        j = k // 2
        dx, dy = lax.rem(j, 4), lax.rem(j // 4 + j, 4)
        far = lax.rem(core + k, 2)
        sign = (2 * far - 1) if source else (1 - 2 * core)
        return lax.rem(x + sign * dx + 4, 4) * 8 + lax.rem(y + sign * dy + 4, 4) * 2 + far

    def peer(k):
        return other(k, False)

    def back(k):
        return other(k, True)

    def cols(i):
        return pl.ds(pl.multiple_of(i * 128, 128), 128)

    hub = nz - 1

    def zpeer(k):
        return lax.rem(z + k, nz)

    load_k = pltpu.make_async_copy(k_hbm, kv, lsem.at[0])
    load_v = pltpu.make_async_copy(v_hbm, vv, lsem.at[1])

    barrier = pltpu.get_barrier_semaphore()

    def greet(k, carry):
        pl.semaphore_signal(barrier, inc=1, device_id={"pack": peer(k)}, device_id_type=MESH)
        return carry

    lax.fori_loop(1, NP, greet, 0)
    load_k.start()
    load_v.start()
    f32 = jnp.float32
    i32 = jnp.int32
    lens_e_r = lens_e_ref[...]
    lens_d_r = lens_d_ref[...]
    ep_r = ep_ref[...]
    dpk_r = dpk_ref[...]
    at_row = lax.broadcasted_iota(i32, (64, 64), 0)
    at_col = lax.broadcasted_iota(i32, (64, 64), 1)

    def column(row):
        return jnp.sum(jnp.where(at_row == at_col, row, 0), axis=1, keepdims=True)

    lens_d_c = column(lens_d_r)
    group = lax.broadcasted_iota(i32, (64, 128), 1)
    part = jnp.sum(jnp.where(column(task_ref[...]) == group, lens_d_c, 0), axis=0, keepdims=True)
    cnt[z] = jnp.broadcast_to(part.astype(f32), (8, 128))

    ahead_e = jnp.where(column(ep_r) == ep_r, jnp.where(at_row < at_col, 1, 0), 0)
    ahead_d = jnp.where(column(dpk_r) == dpk_r, jnp.where(at_row < at_col, 1, 0), 0)
    slot_e_r = 2 * ep_r + jnp.sum(ahead_e, axis=0, keepdims=True)
    slot_d_r = 2 * dpk_r + jnp.sum(ahead_d, axis=0, keepdims=True)
    start_r = 16 * dpk_r + jnp.sum(ahead_d * lens_d_c, axis=0, keepdims=True) // 8

    def pick(slot_r, values_r):
        return jnp.sum(jnp.where(slot_r == at_row, values_r, 0), axis=1, keepdims=True)

    columns = (
        pick(slot_e_r, start_r), pick(slot_e_r, lens_d_r), pick(slot_e_r, lens_e_r), pick(slot_e_r, task_ref[...]),
        pick(slot_d_r, slot_e_r), pick(slot_d_r, lens_d_r),
    )
    wide = jnp.zeros((64, 128), i32)
    for at, values in enumerate(columns):
        wide = jnp.where(group == at, values, wide)
    wide = jnp.concatenate([wide, jnp.zeros((64, 128), i32)], axis=0)
    tab_v[...] = wide.T[:8]
    table_copy = pltpu.make_async_copy(tab_v, tab, lsem.at[5])
    table_copy.start()
    pl.semaphore_wait(barrier, jnp.where(z == hub, NP + nz - 2, NP - 1))

    @pl.when(z != hub)
    def _():
        pl.semaphore_signal(barrier, inc=1, device_id={"dp": hub}, device_id_type=MESH)


    def spread(src, dst, send, recv):
        def make(k):
            return pltpu.make_async_remote_copy(
                src_ref=src.at[:, :, cols(peer(k))],
                dst_ref=dst.at[pl.ds(me * 16, 16)],
                send_sem=send,
                recv_sem=recv,
                device_id={"pack": peer(k)},
                device_id_type=MESH,
            )
        return make

    def run(count_from, body, unroll=False):
        def step(k, carry):
            body(k)
            return carry
        lax.fori_loop(count_from, NP, step, 0, unroll=unroll)

    def total(buffer, send, recv):
        return pltpu.make_async_remote_copy(
            src_ref=buffer, dst_ref=buffer, send_sem=send, recv_sem=recv,
            device_id={"pack": peer(1)}, device_id_type=MESH,
        )

    q1 = spread(q_hbm, qt, s1q, r1q)
    c1 = spread(c_hbm, ct, s1c, r1c)
    own_q = pltpu.make_async_copy(q_hbm.at[:, :, cols(me)], qt.at[pl.ds(me * 16, 16)], lsem.at[2])
    own_c = pltpu.make_async_copy(c_hbm.at[:, :, cols(me)], ct.at[pl.ds(me * 16, 16)], lsem.at[3])
    run(1, lambda k: q1(k).start())
    own_q.start()
    run(1, lambda k: c1(k).start())
    own_c.start()

    @pl.when(z == hub)
    def _():
        def answer(k, carry):
            pl.semaphore_signal(barrier, inc=1, device_id={"dp": zpeer(k)}, device_id_type=MESH)
            return carry
        lax.fori_loop(1, nz, answer, 0)

    qt[pl.ds(TABLE, 16)] = jnp.zeros((16, 8, 128), jnp.bfloat16)
    ct[pl.ds(TABLE, 16)] = jnp.zeros((16, 8, 128), jnp.bfloat16)
    bq[pl.ds(NP * PAIR, 16)] = jnp.zeros((16, 8, 128), jnp.bfloat16)

    def to_hub(buffer, send, recv):
        return pltpu.make_async_remote_copy(
            src_ref=buffer.at[z], dst_ref=buffer.at[z], send_sem=send, recv_sem=recv,
            device_id={"dp": hub}, device_id_type=MESH,
        )

    def from_hub(buffer, send, recv, k):
        return pltpu.make_async_remote_copy(
            src_ref=buffer, dst_ref=buffer, send_sem=send, recv_sem=recv,
            device_id={"dp": zpeer(k)}, device_id_type=MESH,
        )

    def run_z(body):
        def step(k, carry):
            body(k)
            return carry
        lax.fori_loop(1, nz, step, 0)


    def deal(table, send_buf, into, send, recv):
        def make(k):
            return pltpu.make_async_remote_copy(
                src_ref=send_buf.at[k],
                dst_ref=into.at[k],
                send_sem=send,
                recv_sem=recv.at[k],
                device_id={"pack": peer(k)},
                device_id_type=MESH,
            )

        def fill(k, dst):
            p = peer(k)
            for a in range(2):
                start = jnp.clip(tab[0, 2 * p + a], 0, TABLE)
                dst[k, pl.ds(a * SLOT, SLOT)] = table[pl.ds(start, SLOT)]

        return make, fill

    q2, fill_q = deal(qt, sq, qin, s2q, r2q)
    c2, fill_c = deal(ct, sc, cin, s2c, r2c)

    all_q1 = total(qt.at[pl.ds(0, 16 * (NP - 1))], s1q, r1q)
    all_q1.wait_recv()
    own_q.wait()

    table_copy.wait()

    def send_q(k):
        fill_q(k, sq)
        q2(k).start()

    run(1, send_q)
    fill_q(0, qin)

    @pl.when(z != hub)
    def _():
        pl.semaphore_wait(barrier, 1)
        to_hub(cnt, szc, rzc).start()

    all_c1 = total(ct.at[pl.ds(0, 16 * (NP - 1))], s1c, r1c)
    all_c1.wait_recv()
    own_c.wait()

    def send_c(k):
        fill_c(k, sc)
        c2(k).start()

    run(1, send_c)
    fill_c(0, cin)
    load_k.wait()
    load_v.wait()

    len0 = tab[1, 2 * me]
    len1 = tab[1, 2 * me + 1]
    keys0 = tab[2, 2 * me]
    all_counts = total(cnt.at[pl.ds(0, nz - 1)], szc, rzc)

    @pl.when(z == hub)
    def _():
        all_counts.wait_recv()
        ctot[...] = jnp.sum(cnt[...], axis=0)
        run_z(lambda k: from_hub(ctot, szt, rzt, k).start())

    @pl.when(z != hub)
    def _():
        from_hub(ctot, szt, rzt, 1).wait_recv()

    counts = ctot[:1]
    lane_r = lax.broadcasted_iota(jnp.int32, (1, 128), 1)
    weights = jnp.concatenate([dro_ref[...].astype(f32), jnp.zeros((1, 128 - GROUPS), f32)], axis=1)
    scales = weights / jnp.sum(weights, axis=1, keepdims=True) * (128.0 * NP * nz / counts)
    own0 = lane_r == tab[3, 2 * me]
    own1 = lane_r == tab[3, 2 * me + 1]
    scale0 = jnp.sum(jnp.where(own0, scales, 0.0), axis=1, keepdims=True)
    scale1 = jnp.sum(jnp.where(own1, scales, 0.0), axis=1, keepdims=True)
    place_c = lax.broadcasted_iota(jnp.int32, (256, 1), 0)
    place_r = lax.broadcasted_iota(jnp.int32, (1, 256), 1)

    def valid_of(place):
        return jnp.where(place < 120, place < len0, place - 120 < len1)

    scale_c = jnp.where(place_c < 120, scale0, scale1)
    scale_r = jnp.where(place_r < 120, scale0, scale1)
    live_c = jnp.where(place_c < 120, jnp.where(place_c < len0, 1.0, 0.0), jnp.where(place_c - 120 < len1, 1.0, 0.0))
    live_r = jnp.where(place_r < 120, jnp.where(place_r < len0, 1.0, 0.0), jnp.where(place_r - 120 < len1, 1.0, 0.0))
    live_c2 = jnp.broadcast_to(live_c, (256, 128)) > 0.5
    live_r2 = jnp.broadcast_to(live_r, (128, 256)) > 0.5
    lane = lax.broadcasted_iota(jnp.int32, (256, 128), 1)
    key_place = lax.broadcasted_iota(jnp.int32, (256, 256), 0)
    query_place = lax.broadcasted_iota(jnp.int32, (256, 256), 1)
    bias = jnp.where(
        jnp.where(query_place < 120, key_place, keys0) < jnp.where(query_place < 120, keys0, key_place + 1),
        0.0, -1e30,
    ).astype(jnp.float32)
    nt = (((1,), (1,)), ((), ()))
    nn = (((1,), (0,)), ((), ()))

    def dot(a, b, dims):
        return lax.dot_general(a, b, dims, preferred_element_type=jnp.float32)

    def flat(ref, k):
        block = ref[k].astype(jnp.float32).reshape(240, 128)
        return jnp.concatenate([block, jnp.zeros((16, 128), jnp.float32)], axis=0)

    def d3(k):
        return pltpu.make_async_remote_copy(
            src_ref=sd.at[k],
            dst_ref=bq.at[pl.ds(me * PAIR, PAIR)],
            send_sem=s3,
            recv_sem=r3,
            device_id={"pack": back(k)},
            device_id_type=MESH,
        )

    def compute(k, loss):
        i = back(k)
        q = flat(qin, k)
        c = flat(cin, k)
        kb = kv[:, cols(i)]
        vb = vv[:, cols(i)]
        k_t = kb.T
        v_t = vb.T
        c_t = c.T
        u = jnp.where(live_c2, (c * scale_c).astype(jnp.bfloat16).astype(jnp.float32), 0.0)
        u_t = jnp.where(live_r2, (c_t * scale_r).astype(jnp.bfloat16).astype(jnp.float32), 0.0)
        dk = jnp.zeros((256, 128), jnp.float32)
        dv = jnp.zeros((256, 128), jnp.float32)
        dq_parts = []
        for h in range(2):
            own = (lane < 64) if h == 0 else (lane >= 64)
            q_h = jnp.where(own, q, 0.0).astype(jnp.bfloat16)
            u_h = jnp.where(own, u, 0.0).astype(jnp.bfloat16)
            scores = dot(kb, q_h, nt) + bias
            highest = jnp.max(scores, axis=0, keepdims=True)
            powers = jnp.exp(scores - highest)
            attention = powers * (1.0 / jnp.sum(powers, axis=0, keepdims=True))
            low = attention.astype(jnp.bfloat16)
            attended = dot(v_t[h * 64:(h + 1) * 64], low, nn).astype(jnp.bfloat16).astype(jnp.float32)
            loss = loss + jnp.sum(attended * c_t[h * 64:(h + 1) * 64], axis=0, keepdims=True)
            drift = jnp.sum(attended * u_t[h * 64:(h + 1) * 64], axis=0, keepdims=True)
            dv = dv + dot(low, u_h, nn)
            grad = dot(vb, u_h, nt)
            ds = (attention * (grad - drift)).astype(jnp.bfloat16)
            dq_parts.append(dot(k_t[h * 64:(h + 1) * 64], ds, nn))
            dk = dk + dot(ds, q_h, nn)
        dq = jnp.concatenate(dq_parts, axis=0).T
        dk_out[:, cols(i)] = dk.astype(jnp.bfloat16)
        dv_out[:, cols(i)] = dv.astype(jnp.bfloat16)
        sd_block = dq[:240].reshape(PAIR, 8, 128).astype(jnp.bfloat16)
        return sd_block, loss

    own_b = pltpu.make_async_copy(sd.at[0], bq.at[pl.ds(me * PAIR, PAIR)], lsem.at[6])

    def pair_step(k, loss):
        @pl.when(k > 0)
        def _():
            q2(k).wait_recv()
            c2(k).wait_recv()

        block, loss = compute(k, loss)
        sd[k] = block

        @pl.when(k > 0)
        def _():
            d3(k).start()

        @pl.when(k == 0)
        def _():
            own_b.start()

        return loss

    loss = lax.fori_loop(0, NP, pair_step, jnp.zeros((1, 256), jnp.float32))
    own_b.wait()
    loss = jnp.where(live_r > 0.5, loss, 0.0)
    loss0 = jnp.sum(jnp.where(place_r < 120, loss, 0.0), axis=1, keepdims=True)
    loss1 = jnp.sum(jnp.where(place_r < 120, 0.0, loss), axis=1, keepdims=True)
    own_loss = jnp.where(own0, loss0, 0.0) + jnp.where(own1, loss1, 0.0)
    lpart[me] = jnp.broadcast_to(own_loss, (8, 128))

    def loss_copy(k):
        return pltpu.make_async_remote_copy(
            src_ref=lpart.at[me],
            dst_ref=lpart.at[me],
            send_sem=sl,
            recv_sem=rl,
            device_id={"pack": peer(k)},
            device_id_type=MESH,
        )

    run(1, lambda k: loss_copy(k).start())

    all_d3 = total(bq.at[pl.ds(0, PAIR * (NP - 1))], s3, r3)
    all_d3.wait_recv()

    def d4(k):
        return pltpu.make_async_remote_copy(
            src_ref=dp.at[k],
            dst_ref=dq_out.at[:, :, cols(me)],
            send_sem=s4,
            recv_sem=r4,
            device_id={"pack": peer(k)},
            device_id_type=MESH,
        )

    own_d = pltpu.make_async_copy(dp.at[0], dq_out.at[:, :, cols(me)], lsem.at[4])

    def fill_d(k):
        d = peer(k)
        near = tab[4, 2 * d] * SLOT
        count = tab[5, 2 * d] // 8
        far = tab[4, 2 * d + 1] * SLOT - count
        for b in range(16):
            dp[k, b] = bq[jnp.clip(jnp.where(b < count, near, far) + b, 0, NP * PAIR - 1)]

    def send_d(k):
        fill_d(k)
        d4(k).start()

    run(1, send_d)
    fill_d(0)
    own_d.start()

    all_loss = total(lpart.at[pl.ds(0, NP - 1)], sl, rl)
    all_loss.wait_recv()
    lz[z] = jnp.sum(lpart[...], axis=0)

    all_zloss = total(lz.at[pl.ds(0, nz - 1)], szl, rzl)

    @pl.when(z == hub)
    def _():
        all_zloss.wait_recv()
        ltot[...] = jnp.sum(lz[...], axis=0)
        run_z(lambda k: from_hub(ltot, szm, rzm, k).start())

    @pl.when(z != hub)
    def _():
        to_hub(lz, szl, rzl).start()
        from_hub(ltot, szm, rzm, 1).wait_recv()

    mean_loss = ltot[:1] / counts
    loss_out[...] = mean_loss[:, :GROUPS]


    @pl.when(z == hub)
    def _():
        total(cnt.at[pl.ds(0, nz - 1)], szt, rzt).wait_send()
        total(lz.at[pl.ds(0, nz - 1)], szm, rzm).wait_send()

    @pl.when(z != hub)
    def _():
        to_hub(cnt, szc, rzc).wait_send()
        to_hub(lz, szl, rzl).wait_send()

    all_loss.wait_send()
    all_q1.wait_send()
    all_c1.wait_send()
    total(sq.at[pl.ds(0, NP - 1)], s2q, r2q.at[0]).wait_send()
    total(sc.at[pl.ds(0, NP - 1)], s2c, r2c.at[0]).wait_send()
    all_d3.wait_send()
    own_d.wait()
    total(dp.at[pl.ds(0, NP - 1)], s4, r4).wait_send()
    total(dp.at[pl.ds(0, NP - 1)], s4, r4).wait_recv()


def local(
    enc_keys, enc_values, dec_queries, cotangent,
    input_lengths, target_lengths, enc_pack, dec_pack, task_group, dro_weights,
):
    bf = jnp.bfloat16
    vmem = pl.BlockSpec(memory_space=pltpu.VMEM)
    hbm = pl.BlockSpec(memory_space=pl.ANY)
    nz = lax.axis_size("dp")
    dma = pltpu.SemaphoreType.DMA
    dq, dk, dv, loss = pl.pallas_call(
        kernel,
        out_shape=(
            pltpu.VMEM((16, 8, 4096), bf),
            pltpu.VMEM((256, 4096), bf),
            pltpu.VMEM((256, 4096), bf),
            pltpu.VMEM((1, GROUPS), jnp.float32),
        ),
        in_specs=[vmem] * 6 + [hbm] * 4,
        out_specs=(vmem, vmem, vmem, vmem),
        scratch_shapes=[
            pltpu.VMEM((256, 4096), bf),
            pltpu.VMEM((256, 4096), bf),
            pltpu.VMEM((TABLE + 16, 8, 128), bf),
            pltpu.VMEM((TABLE + 16, 8, 128), bf),
            pltpu.VMEM((NP, PAIR, 8, 128), bf),
            pltpu.VMEM((NP, PAIR, 8, 128), bf),
            pltpu.VMEM((NP, PAIR, 8, 128), bf),
            pltpu.VMEM((NP, PAIR, 8, 128), bf),
            pltpu.VMEM((NP, PAIR, 8, 128), bf),
            pltpu.VMEM((NP * PAIR + 16, 8, 128), bf),
            pltpu.VMEM((NP, 16, 8, 128), bf),
            pltpu.VMEM((8, 128), jnp.int32),
            pltpu.SMEM((8, 128), jnp.int32),
            pltpu.VMEM((nz, 8, 128), jnp.float32),
            pltpu.VMEM((NP, 8, 128), jnp.float32),
            pltpu.VMEM((nz, 8, 128), jnp.float32),
            pltpu.VMEM((8, 128), jnp.float32),
            pltpu.VMEM((8, 128), jnp.float32),
            dma((8,)),
            dma((20,)),
            dma((NP,)),
            dma((NP,)),
        ],
        compiler_params=pltpu.CompilerParams(
            collective_id=0, has_side_effects=True, vmem_limit_bytes=56 * 1024 * 1024
        ),
        cost_estimate=pl.CostEstimate(flops=3_000_000_000, bytes_accessed=11_000_000, transcendentals=4_000_000),
    )(
        input_lengths, target_lengths, enc_pack, dec_pack, task_group.reshape(1, 64), dro_weights.reshape(1, GROUPS),
        enc_keys, enc_values,
        dec_queries.reshape(16, 8, 4096), cotangent.reshape(16, 8, 4096),
    )
    return dq.reshape(128, 4096), dk, dv, loss.reshape(GROUPS)


def solution(mesh):
    rows = P(("dp", "pack"), None)
    small = P("dp", None)
    return jax.shard_map(
        local,
        mesh=mesh,
        in_specs=(rows, rows, rows, rows, small, small, small, small, P("dp", None, None), P()),
        out_specs=(rows, rows, rows, P()),
        check_vma=False,
    )
```

```python
import functools

import jax
import jax.numpy as jnp
from jax import lax
from jax.experimental import pallas as pl
from jax.experimental.pallas import tpu as pltpu
from jax.sharding import PartitionSpec as P

HEAD_DIM = 64
GROUPS = 16
NP = 32
SLOT = 15
PAIR = 2 * SLOT
TABLE = NP * 16
MESH = pl.DeviceIdType.MESH


def kernel(
    lens_e_ref, lens_d_ref, ep_ref, dpk_ref, task_ref, dro_ref,
    k_hbm, v_hbm, q_hbm, c_hbm,
    dq_out, dk_out, dv_out, loss_out,
    kv, vv, qt, ct, sq, sc, qin, cin, sd, bq, dp,
    tab_v, tab, cnt, lpart, lz, ctot, ltot,
    lsem, one, r2q, r2c,
):
    s1q, r1q, s1c, r1c, s2q, s2c, s3, r3, s4, r4, sl, rl, szc, rzc, szl, rzl, szt, rzt, szm, rzm = (
        one.at[at] for at in range(20)
    )
    me = lax.axis_index("pack")
    z = lax.axis_index("dp")
    nz = lax.axis_size("dp")
    x, y, core = me // 8, lax.rem(me // 2, 4), lax.rem(me, 2)

    def other(k, source):
        j = lax.rem(k, 16)
        d0, d1 = lax.rem(j, 4), lax.rem(j // 4 + j, 4)
        far = lax.rem(core + k // 16, 2)
        turn = far if source else core
        dx = d0 + turn * (d1 - d0)
        dy = d1 + turn * (d0 - d1)
        sign = -1 if source else 1
        return lax.rem(x + sign * dx + 4, 4) * 8 + lax.rem(y + sign * dy + 4, 4) * 2 + far

    def peer(k):
        return other(k, False)

    def back(k):
        return other(k, True)

    def cols(i):
        return pl.ds(pl.multiple_of(i * 128, 128), 128)

    hub = nz - 1

    def zpeer(k):
        return lax.rem(z + k, nz)

    load_k = pltpu.make_async_copy(k_hbm, kv, lsem.at[0])
    load_v = pltpu.make_async_copy(v_hbm, vv, lsem.at[1])

    barrier = pltpu.get_barrier_semaphore()

    def greet(k, carry):
        pl.semaphore_signal(barrier, inc=1, device_id={"pack": peer(k)}, device_id_type=MESH)
        return carry

    lax.fori_loop(1, NP, greet, 0)
    load_k.start()
    load_v.start()
    f32 = jnp.float32
    i32 = jnp.int32
    pl.semaphore_wait(barrier, jnp.where(z == hub, NP + nz - 2, NP - 1))

    @pl.when(z != hub)
    def _():
        pl.semaphore_signal(barrier, inc=1, device_id={"dp": hub}, device_id_type=MESH)


    def spread(src, dst, send, recv):
        def make(k):
            return pltpu.make_async_remote_copy(
                src_ref=src.at[:, :, cols(peer(k))],
                dst_ref=dst.at[pl.ds(me * 16, 16)],
                send_sem=send,
                recv_sem=recv,
                device_id={"pack": peer(k)},
                device_id_type=MESH,
            )
        return make

    def run(count_from, body, unroll=False):
        def step(k, carry):
            body(k)
            return carry
        lax.fori_loop(count_from, NP, step, 0, unroll=unroll)

    def total(buffer, send, recv):
        return pltpu.make_async_remote_copy(
            src_ref=buffer, dst_ref=buffer, send_sem=send, recv_sem=recv,
            device_id={"pack": peer(1)}, device_id_type=MESH,
        )

    q1 = spread(q_hbm, qt, s1q, r1q)
    c1 = spread(c_hbm, ct, s1c, r1c)
    own_q = pltpu.make_async_copy(q_hbm.at[:, :, cols(me)], qt.at[pl.ds(me * 16, 16)], lsem.at[2])
    own_c = pltpu.make_async_copy(c_hbm.at[:, :, cols(me)], ct.at[pl.ds(me * 16, 16)], lsem.at[3])
    run(1, lambda k: q1(k).start())
    own_q.start()
    run(1, lambda k: c1(k).start())
    own_c.start()

    @pl.when(z == hub)
    def _():
        def answer(k, carry):
            pl.semaphore_signal(barrier, inc=1, device_id={"dp": zpeer(k)}, device_id_type=MESH)
            return carry
        lax.fori_loop(1, nz, answer, 0)

    lens_e_r = lens_e_ref[...]
    lens_d_r = lens_d_ref[...]
    ep_r = ep_ref[...]
    dpk_r = dpk_ref[...]
    at_row = lax.broadcasted_iota(i32, (64, 64), 0)
    at_col = lax.broadcasted_iota(i32, (64, 64), 1)

    def column(row):
        return jnp.sum(jnp.where(at_row == at_col, row, 0), axis=1, keepdims=True)

    lens_d_c = column(lens_d_r)
    group = lax.broadcasted_iota(i32, (64, 128), 1)
    part = jnp.sum(jnp.where(column(task_ref[...]) == group, lens_d_c, 0), axis=0, keepdims=True)
    cnt[z] = jnp.broadcast_to(part.astype(f32), (8, 128))

    ahead_e = jnp.where(column(ep_r) == ep_r, jnp.where(at_row < at_col, 1, 0), 0)
    ahead_d = jnp.where(column(dpk_r) == dpk_r, jnp.where(at_row < at_col, 1, 0), 0)
    slot_e_r = 2 * ep_r + jnp.sum(ahead_e, axis=0, keepdims=True)
    slot_d_r = 2 * dpk_r + jnp.sum(ahead_d, axis=0, keepdims=True)
    start_r = 16 * dpk_r + jnp.sum(ahead_d * lens_d_c, axis=0, keepdims=True) // 8

    def pick(slot_r, values_r):
        return jnp.sum(jnp.where(slot_r == at_row, values_r, 0), axis=1, keepdims=True)

    columns = (
        pick(slot_e_r, start_r), pick(slot_e_r, lens_d_r), pick(slot_e_r, lens_e_r), pick(slot_e_r, task_ref[...]),
        pick(slot_d_r, slot_e_r), pick(slot_d_r, lens_d_r),
    )
    wide = jnp.zeros((64, 128), i32)
    for at, values in enumerate(columns):
        wide = jnp.where(group == at, values, wide)
    wide = jnp.concatenate([wide, jnp.zeros((64, 128), i32)], axis=0)
    tab_v[...] = wide.T[:8]
    table_copy = pltpu.make_async_copy(tab_v, tab, lsem.at[5])
    table_copy.start()
    qt[pl.ds(TABLE, 16)] = jnp.zeros((16, 8, 128), jnp.bfloat16)
    ct[pl.ds(TABLE, 16)] = jnp.zeros((16, 8, 128), jnp.bfloat16)
    bq[pl.ds(NP * PAIR, 16)] = jnp.zeros((16, 8, 128), jnp.bfloat16)

    def to_hub(buffer, send, recv):
        return pltpu.make_async_remote_copy(
            src_ref=buffer.at[z], dst_ref=buffer.at[z], send_sem=send, recv_sem=recv,
            device_id={"dp": hub}, device_id_type=MESH,
        )

    def from_hub(buffer, send, recv, k):
        return pltpu.make_async_remote_copy(
            src_ref=buffer, dst_ref=buffer, send_sem=send, recv_sem=recv,
            device_id={"dp": zpeer(k)}, device_id_type=MESH,
        )

    def run_z(body):
        def step(k, carry):
            body(k)
            return carry
        lax.fori_loop(1, nz, step, 0)


    def deal(table, send_buf, into, send, recv):
        def make(k):
            return pltpu.make_async_remote_copy(
                src_ref=send_buf.at[k],
                dst_ref=into.at[k],
                send_sem=send,
                recv_sem=recv.at[k],
                device_id={"pack": peer(k)},
                device_id_type=MESH,
            )

        def fill(k, dst):
            p = peer(k)
            for a in range(2):
                start = jnp.clip(tab[0, 2 * p + a], 0, TABLE)
                dst[k, pl.ds(a * SLOT, SLOT)] = table[pl.ds(start, SLOT)]

        return make, fill

    q2, fill_q = deal(qt, sq, qin, s2q, r2q)
    c2, fill_c = deal(ct, sc, cin, s2c, r2c)

    all_q1 = total(qt.at[pl.ds(0, 16 * (NP - 1))], s1q, r1q)
    all_q1.wait_recv()
    own_q.wait()

    table_copy.wait()

    def send_q(k):
        fill_q(k, sq)
        q2(k).start()

    run(1, send_q)
    fill_q(0, qin)

    @pl.when(z != hub)
    def _():
        pl.semaphore_wait(barrier, 1)
        to_hub(cnt, szc, rzc).start()

    all_c1 = total(ct.at[pl.ds(0, 16 * (NP - 1))], s1c, r1c)
    all_c1.wait_recv()
    own_c.wait()

    def send_c(k):
        fill_c(k, sc)
        c2(k).start()

    run(1, send_c)
    fill_c(0, cin)
    load_k.wait()
    load_v.wait()

    len0 = tab[1, 2 * me]
    len1 = tab[1, 2 * me + 1]
    keys0 = tab[2, 2 * me]
    all_counts = total(cnt.at[pl.ds(0, nz - 1)], szc, rzc)

    @pl.when(z == hub)
    def _():
        all_counts.wait_recv()
        ctot[...] = jnp.sum(cnt[...], axis=0)
        run_z(lambda k: from_hub(ctot, szt, rzt, k).start())

    @pl.when(z != hub)
    def _():
        from_hub(ctot, szt, rzt, 1).wait_recv()

    counts = ctot[:1]
    lane_r = lax.broadcasted_iota(jnp.int32, (1, 128), 1)
    weights = jnp.concatenate([dro_ref[...].astype(f32), jnp.zeros((1, 128 - GROUPS), f32)], axis=1)
    scales = weights / jnp.sum(weights, axis=1, keepdims=True) * (128.0 * NP * nz / counts)
    own0 = lane_r == tab[3, 2 * me]
    own1 = lane_r == tab[3, 2 * me + 1]
    scale0 = jnp.sum(jnp.where(own0, scales, 0.0), axis=1, keepdims=True)
    scale1 = jnp.sum(jnp.where(own1, scales, 0.0), axis=1, keepdims=True)
    place_c = lax.broadcasted_iota(jnp.int32, (256, 1), 0)
    place_r = lax.broadcasted_iota(jnp.int32, (1, 256), 1)

    def valid_of(place):
        return jnp.where(place < 120, place < len0, place - 120 < len1)

    scale_c = jnp.where(place_c < 120, scale0, scale1)
    scale_r = jnp.where(place_r < 120, scale0, scale1)
    live_c = jnp.where(place_c < 120, jnp.where(place_c < len0, 1.0, 0.0), jnp.where(place_c - 120 < len1, 1.0, 0.0))
    live_r = jnp.where(place_r < 120, jnp.where(place_r < len0, 1.0, 0.0), jnp.where(place_r - 120 < len1, 1.0, 0.0))
    live_c2 = jnp.broadcast_to(live_c, (256, 128)) > 0.5
    live_r2 = jnp.broadcast_to(live_r, (128, 256)) > 0.5
    lane = lax.broadcasted_iota(jnp.int32, (256, 128), 1)
    key_place = lax.broadcasted_iota(jnp.int32, (256, 256), 0)
    query_place = lax.broadcasted_iota(jnp.int32, (256, 256), 1)
    bias = jnp.where(
        jnp.where(query_place < 120, key_place, keys0) < jnp.where(query_place < 120, keys0, key_place + 1),
        0.0, -1e30,
    ).astype(jnp.float32)
    nt = (((1,), (1,)), ((), ()))
    nn = (((1,), (0,)), ((), ()))

    def dot(a, b, dims):
        return lax.dot_general(a, b, dims, preferred_element_type=jnp.float32)

    def flat(ref, k):
        block = ref[k].astype(jnp.float32).reshape(240, 128)
        return jnp.concatenate([block, jnp.zeros((16, 128), jnp.float32)], axis=0)

    def d3(k):
        return pltpu.make_async_remote_copy(
            src_ref=sd.at[k],
            dst_ref=bq.at[pl.ds(me * PAIR, PAIR)],
            send_sem=s3,
            recv_sem=r3,
            device_id={"pack": back(k)},
            device_id_type=MESH,
        )

    def compute(k, loss):
        i = back(k)
        q = flat(qin, k)
        c = flat(cin, k)
        kb = kv[:, cols(i)]
        vb = vv[:, cols(i)]
        k_t = kb.T
        v_t = vb.T
        c_t = c.T
        u = jnp.where(live_c2, (c * scale_c).astype(jnp.bfloat16).astype(jnp.float32), 0.0)
        u_t = jnp.where(live_r2, (c_t * scale_r).astype(jnp.bfloat16).astype(jnp.float32), 0.0)
        dk = jnp.zeros((256, 128), jnp.float32)
        dv = jnp.zeros((256, 128), jnp.float32)
        dq_parts = []
        for h in range(2):
            own = (lane < 64) if h == 0 else (lane >= 64)
            q_h = jnp.where(own, q, 0.0).astype(jnp.bfloat16)
            u_h = jnp.where(own, u, 0.0).astype(jnp.bfloat16)
            scores = dot(kb, q_h, nt) + bias
            highest = jnp.max(scores, axis=0, keepdims=True)
            powers = jnp.exp(scores - highest)
            attention = powers * (1.0 / jnp.sum(powers, axis=0, keepdims=True))
            low = attention.astype(jnp.bfloat16)
            attended = dot(v_t[h * 64:(h + 1) * 64], low, nn).astype(jnp.bfloat16).astype(jnp.float32)
            loss = loss + jnp.sum(attended * c_t[h * 64:(h + 1) * 64], axis=0, keepdims=True)
            drift = jnp.sum(attended * u_t[h * 64:(h + 1) * 64], axis=0, keepdims=True)
            dv = dv + dot(low, u_h, nn)
            grad = dot(vb, u_h, nt)
            ds = (attention * (grad - drift)).astype(jnp.bfloat16)
            dq_parts.append(dot(k_t[h * 64:(h + 1) * 64], ds, nn))
            dk = dk + dot(ds, q_h, nn)
        dq = jnp.concatenate(dq_parts, axis=0).T
        dk_out[:, cols(i)] = dk.astype(jnp.bfloat16)
        dv_out[:, cols(i)] = dv.astype(jnp.bfloat16)
        sd_block = dq[:240].reshape(PAIR, 8, 128).astype(jnp.bfloat16)
        return sd_block, loss

    own_b = pltpu.make_async_copy(sd.at[0], bq.at[pl.ds(me * PAIR, PAIR)], lsem.at[6])

    def pair_step(k, loss):
        @pl.when(k > 0)
        def _():
            q2(k).wait_recv()
            c2(k).wait_recv()

        block, loss = compute(k, loss)
        sd[k] = block

        @pl.when(k > 0)
        def _():
            d3(k).start()

        @pl.when(k == 0)
        def _():
            own_b.start()

        return loss

    loss = lax.fori_loop(0, NP, pair_step, jnp.zeros((1, 256), jnp.float32))
    own_b.wait()
    loss = jnp.where(live_r > 0.5, loss, 0.0)
    loss0 = jnp.sum(jnp.where(place_r < 120, loss, 0.0), axis=1, keepdims=True)
    loss1 = jnp.sum(jnp.where(place_r < 120, 0.0, loss), axis=1, keepdims=True)
    own_loss = jnp.where(own0, loss0, 0.0) + jnp.where(own1, loss1, 0.0)
    lpart[me] = jnp.broadcast_to(own_loss, (8, 128))

    def loss_copy(k):
        return pltpu.make_async_remote_copy(
            src_ref=lpart.at[me],
            dst_ref=lpart.at[me],
            send_sem=sl,
            recv_sem=rl,
            device_id={"pack": peer(k)},
            device_id_type=MESH,
        )

    run(1, lambda k: loss_copy(k).start())

    all_d3 = total(bq.at[pl.ds(0, PAIR * (NP - 1))], s3, r3)
    all_d3.wait_recv()

    def d4(k):
        return pltpu.make_async_remote_copy(
            src_ref=dp.at[k],
            dst_ref=dq_out.at[:, :, cols(me)],
            send_sem=s4,
            recv_sem=r4,
            device_id={"pack": peer(k)},
            device_id_type=MESH,
        )

    own_d = pltpu.make_async_copy(dp.at[0], dq_out.at[:, :, cols(me)], lsem.at[4])

    def fill_d(k):
        d = peer(k)
        near = tab[4, 2 * d] * SLOT
        count = tab[5, 2 * d] // 8
        far = tab[4, 2 * d + 1] * SLOT - count
        for b in range(16):
            dp[k, b] = bq[jnp.clip(jnp.where(b < count, near, far) + b, 0, NP * PAIR - 1)]

    def send_d(k):
        fill_d(k)
        d4(k).start()

    run(1, send_d)
    fill_d(0)
    own_d.start()

    all_loss = total(lpart.at[pl.ds(0, NP - 1)], sl, rl)
    all_loss.wait_recv()
    lz[z] = jnp.sum(lpart[...], axis=0)

    all_zloss = total(lz.at[pl.ds(0, nz - 1)], szl, rzl)

    @pl.when(z == hub)
    def _():
        all_zloss.wait_recv()
        ltot[...] = jnp.sum(lz[...], axis=0)
        run_z(lambda k: from_hub(ltot, szm, rzm, k).start())

    @pl.when(z != hub)
    def _():
        to_hub(lz, szl, rzl).start()
        from_hub(ltot, szm, rzm, 1).wait_recv()

    mean_loss = ltot[:1] / counts
    loss_out[...] = mean_loss[:, :GROUPS]


    @pl.when(z == hub)
    def _():
        total(cnt.at[pl.ds(0, nz - 1)], szt, rzt).wait_send()
        total(lz.at[pl.ds(0, nz - 1)], szm, rzm).wait_send()

    @pl.when(z != hub)
    def _():
        to_hub(cnt, szc, rzc).wait_send()
        to_hub(lz, szl, rzl).wait_send()

    all_loss.wait_send()
    all_q1.wait_send()
    all_c1.wait_send()
    total(sq.at[pl.ds(0, NP - 1)], s2q, r2q.at[0]).wait_send()
    total(sc.at[pl.ds(0, NP - 1)], s2c, r2c.at[0]).wait_send()
    all_d3.wait_send()
    own_d.wait()
    total(dp.at[pl.ds(0, NP - 1)], s4, r4).wait_send()
    total(dp.at[pl.ds(0, NP - 1)], s4, r4).wait_recv()


def local(
    enc_keys, enc_values, dec_queries, cotangent,
    input_lengths, target_lengths, enc_pack, dec_pack, task_group, dro_weights,
):
    bf = jnp.bfloat16
    vmem = pl.BlockSpec(memory_space=pltpu.VMEM)
    hbm = pl.BlockSpec(memory_space=pl.ANY)
    nz = lax.axis_size("dp")
    dma = pltpu.SemaphoreType.DMA
    dq, dk, dv, loss = pl.pallas_call(
        kernel,
        out_shape=(
            pltpu.VMEM((16, 8, 4096), bf),
            pltpu.VMEM((256, 4096), bf),
            pltpu.VMEM((256, 4096), bf),
            pltpu.VMEM((1, GROUPS), jnp.float32),
        ),
        in_specs=[vmem] * 6 + [hbm] * 4,
        out_specs=(vmem, vmem, vmem, vmem),
        scratch_shapes=[
            pltpu.VMEM((256, 4096), bf),
            pltpu.VMEM((256, 4096), bf),
            pltpu.VMEM((TABLE + 16, 8, 128), bf),
            pltpu.VMEM((TABLE + 16, 8, 128), bf),
            pltpu.VMEM((NP, PAIR, 8, 128), bf),
            pltpu.VMEM((NP, PAIR, 8, 128), bf),
            pltpu.VMEM((NP, PAIR, 8, 128), bf),
            pltpu.VMEM((NP, PAIR, 8, 128), bf),
            pltpu.VMEM((NP, PAIR, 8, 128), bf),
            pltpu.VMEM((NP * PAIR + 16, 8, 128), bf),
            pltpu.VMEM((NP, 16, 8, 128), bf),
            pltpu.VMEM((8, 128), jnp.int32),
            pltpu.SMEM((8, 128), jnp.int32),
            pltpu.VMEM((nz, 8, 128), jnp.float32),
            pltpu.VMEM((NP, 8, 128), jnp.float32),
            pltpu.VMEM((nz, 8, 128), jnp.float32),
            pltpu.VMEM((8, 128), jnp.float32),
            pltpu.VMEM((8, 128), jnp.float32),
            dma((8,)),
            dma((20,)),
            dma((NP,)),
            dma((NP,)),
        ],
        compiler_params=pltpu.CompilerParams(
            collective_id=0, has_side_effects=True, vmem_limit_bytes=56 * 1024 * 1024
        ),
        cost_estimate=pl.CostEstimate(flops=3_000_000_000, bytes_accessed=11_000_000, transcendentals=4_000_000),
    )(
        input_lengths, target_lengths, enc_pack, dec_pack, task_group.reshape(1, 64), dro_weights.reshape(1, GROUPS),
        enc_keys, enc_values,
        dec_queries.reshape(16, 8, 4096), cotangent.reshape(16, 8, 4096),
    )
    return dq.reshape(128, 4096), dk, dv, loss.reshape(GROUPS)


def solution(mesh):
    rows = P(("dp", "pack"), None)
    small = P("dp", None)
    return jax.shard_map(
        local,
        mesh=mesh,
        in_specs=(rows, rows, rows, rows, small, small, small, small, P("dp", None, None), P()),
        out_specs=(rows, rows, rows, P()),
        check_vma=False,
    )
```

```python
import functools

import jax
import jax.numpy as jnp
from jax import lax
from jax.experimental import pallas as pl
from jax.experimental.pallas import tpu as pltpu
from jax.sharding import PartitionSpec as P

HEAD_DIM = 64
GROUPS = 16
NP = 32
SLOT = 15
PAIR = 2 * SLOT
TABLE = NP * 16
MESH = pl.DeviceIdType.MESH


def kernel(
    lens_e_ref, lens_d_ref, ep_ref, dpk_ref, task_ref, dro_ref,
    k_hbm, v_hbm, q_hbm, c_hbm,
    dq_out, dk_out, dv_out, loss_out,
    kv, vv, qt, ct, sq, sc, qin, cin, sd, bq, dp,
    tab_v, tab, cnt, lpart, lz, ctot, ltot,
    lsem, one, r2q, r2c,
):
    s1q, r1q, s1c, r1c, s2q, s2c, s3, r3, s4, r4, sl, rl, szc, rzc, szl, rzl, szt, rzt, szm, rzm = (
        one.at[at] for at in range(20)
    )
    me = lax.axis_index("pack")
    z = lax.axis_index("dp")
    nz = lax.axis_size("dp")
    x, y, core = me // 8, lax.rem(me // 2, 4), lax.rem(me, 2)

    def other(k, source):
        j = lax.rem(k, 16)
        d0, d1 = lax.rem(j, 4), lax.rem(j // 4 + j, 4)
        far = lax.rem(core + k // 16, 2)
        turn = far if source else core
        dx = d0 + turn * (4 - d1 - d0)
        dy = d1 + turn * (d0 - d1)
        sign = -1 if source else 1
        return lax.rem(x + sign * dx + 8, 4) * 8 + lax.rem(y + sign * dy + 8, 4) * 2 + far

    def peer(k):
        return other(k, False)

    def back(k):
        return other(k, True)

    def cols(i):
        return pl.ds(pl.multiple_of(i * 128, 128), 128)

    hub = nz - 1

    def zpeer(k):
        return lax.rem(z + k, nz)

    load_k = pltpu.make_async_copy(k_hbm, kv, lsem.at[0])
    load_v = pltpu.make_async_copy(v_hbm, vv, lsem.at[1])

    barrier = pltpu.get_barrier_semaphore()

    def greet(k, carry):
        pl.semaphore_signal(barrier, inc=1, device_id={"pack": peer(k)}, device_id_type=MESH)
        return carry

    lax.fori_loop(1, NP, greet, 0)
    load_k.start()
    load_v.start()
    f32 = jnp.float32
    i32 = jnp.int32
    pl.semaphore_wait(barrier, jnp.where(z == hub, NP + nz - 2, NP - 1))

    @pl.when(z != hub)
    def _():
        pl.semaphore_signal(barrier, inc=1, device_id={"dp": hub}, device_id_type=MESH)


    def spread(src, dst, send, recv):
        def make(k):
            return pltpu.make_async_remote_copy(
                src_ref=src.at[:, :, cols(peer(k))],
                dst_ref=dst.at[pl.ds(me * 16, 16)],
                send_sem=send,
                recv_sem=recv,
                device_id={"pack": peer(k)},
                device_id_type=MESH,
            )
        return make

    def run(count_from, body, unroll=False):
        def step(k, carry):
            body(k)
            return carry
        lax.fori_loop(count_from, NP, step, 0, unroll=unroll)

    def total(buffer, send, recv):
        return pltpu.make_async_remote_copy(
            src_ref=buffer, dst_ref=buffer, send_sem=send, recv_sem=recv,
            device_id={"pack": peer(1)}, device_id_type=MESH,
        )

    q1 = spread(q_hbm, qt, s1q, r1q)
    c1 = spread(c_hbm, ct, s1c, r1c)
    own_q = pltpu.make_async_copy(q_hbm.at[:, :, cols(me)], qt.at[pl.ds(me * 16, 16)], lsem.at[2])
    own_c = pltpu.make_async_copy(c_hbm.at[:, :, cols(me)], ct.at[pl.ds(me * 16, 16)], lsem.at[3])
    run(1, lambda k: q1(k).start())
    own_q.start()
    run(1, lambda k: c1(k).start())
    own_c.start()

    @pl.when(z == hub)
    def _():
        def answer(k, carry):
            pl.semaphore_signal(barrier, inc=1, device_id={"dp": zpeer(k)}, device_id_type=MESH)
            return carry
        lax.fori_loop(1, nz, answer, 0)

    lens_e_r = lens_e_ref[...]
    lens_d_r = lens_d_ref[...]
    ep_r = ep_ref[...]
    dpk_r = dpk_ref[...]
    at_row = lax.broadcasted_iota(i32, (64, 64), 0)
    at_col = lax.broadcasted_iota(i32, (64, 64), 1)

    def column(row):
        return jnp.sum(jnp.where(at_row == at_col, row, 0), axis=1, keepdims=True)

    lens_d_c = column(lens_d_r)
    group = lax.broadcasted_iota(i32, (64, 128), 1)
    part = jnp.sum(jnp.where(column(task_ref[...]) == group, lens_d_c, 0), axis=0, keepdims=True)
    cnt[z] = jnp.broadcast_to(part.astype(f32), (8, 128))

    ahead_e = jnp.where(column(ep_r) == ep_r, jnp.where(at_row < at_col, 1, 0), 0)
    ahead_d = jnp.where(column(dpk_r) == dpk_r, jnp.where(at_row < at_col, 1, 0), 0)
    slot_e_r = 2 * ep_r + jnp.sum(ahead_e, axis=0, keepdims=True)
    slot_d_r = 2 * dpk_r + jnp.sum(ahead_d, axis=0, keepdims=True)
    start_r = 16 * dpk_r + jnp.sum(ahead_d * lens_d_c, axis=0, keepdims=True) // 8

    def pick(slot_r, values_r):
        return jnp.sum(jnp.where(slot_r == at_row, values_r, 0), axis=1, keepdims=True)

    columns = (
        pick(slot_e_r, start_r), pick(slot_e_r, lens_d_r), pick(slot_e_r, lens_e_r), pick(slot_e_r, task_ref[...]),
        pick(slot_d_r, slot_e_r), pick(slot_d_r, lens_d_r),
    )
    wide = jnp.zeros((64, 128), i32)
    for at, values in enumerate(columns):
        wide = jnp.where(group == at, values, wide)
    wide = jnp.concatenate([wide, jnp.zeros((64, 128), i32)], axis=0)
    tab_v[...] = wide.T[:8]
    table_copy = pltpu.make_async_copy(tab_v, tab, lsem.at[5])
    table_copy.start()
    qt[pl.ds(TABLE, 16)] = jnp.zeros((16, 8, 128), jnp.bfloat16)
    ct[pl.ds(TABLE, 16)] = jnp.zeros((16, 8, 128), jnp.bfloat16)
    bq[pl.ds(NP * PAIR, 16)] = jnp.zeros((16, 8, 128), jnp.bfloat16)

    def to_hub(buffer, send, recv):
        return pltpu.make_async_remote_copy(
            src_ref=buffer.at[z], dst_ref=buffer.at[z], send_sem=send, recv_sem=recv,
            device_id={"dp": hub}, device_id_type=MESH,
        )

    def from_hub(buffer, send, recv, k):
        return pltpu.make_async_remote_copy(
            src_ref=buffer, dst_ref=buffer, send_sem=send, recv_sem=recv,
            device_id={"dp": zpeer(k)}, device_id_type=MESH,
        )

    def run_z(body):
        def step(k, carry):
            body(k)
            return carry
        lax.fori_loop(1, nz, step, 0)


    def deal(table, send_buf, into, send, recv):
        def make(k):
            return pltpu.make_async_remote_copy(
                src_ref=send_buf.at[k],
                dst_ref=into.at[k],
                send_sem=send,
                recv_sem=recv.at[k],
                device_id={"pack": peer(k)},
                device_id_type=MESH,
            )

        def fill(k, dst):
            p = peer(k)
            for a in range(2):
                start = jnp.clip(tab[0, 2 * p + a], 0, TABLE)
                dst[k, pl.ds(a * SLOT, SLOT)] = table[pl.ds(start, SLOT)]

        return make, fill

    q2, fill_q = deal(qt, sq, qin, s2q, r2q)
    c2, fill_c = deal(ct, sc, cin, s2c, r2c)

    all_q1 = total(qt.at[pl.ds(0, 16 * (NP - 1))], s1q, r1q)
    all_q1.wait_recv()
    own_q.wait()

    table_copy.wait()

    def send_q(k):
        fill_q(k, sq)
        q2(k).start()

    run(1, send_q)
    fill_q(0, qin)

    @pl.when(z != hub)
    def _():
        pl.semaphore_wait(barrier, 1)
        to_hub(cnt, szc, rzc).start()

    all_c1 = total(ct.at[pl.ds(0, 16 * (NP - 1))], s1c, r1c)
    all_c1.wait_recv()
    own_c.wait()

    def send_c(k):
        fill_c(k, sc)
        c2(k).start()

    run(1, send_c)
    fill_c(0, cin)
    load_k.wait()
    load_v.wait()

    len0 = tab[1, 2 * me]
    len1 = tab[1, 2 * me + 1]
    keys0 = tab[2, 2 * me]
    all_counts = total(cnt.at[pl.ds(0, nz - 1)], szc, rzc)

    @pl.when(z == hub)
    def _():
        all_counts.wait_recv()
        ctot[...] = jnp.sum(cnt[...], axis=0)
        run_z(lambda k: from_hub(ctot, szt, rzt, k).start())

    @pl.when(z != hub)
    def _():
        from_hub(ctot, szt, rzt, 1).wait_recv()

    counts = ctot[:1]
    lane_r = lax.broadcasted_iota(jnp.int32, (1, 128), 1)
    weights = jnp.concatenate([dro_ref[...].astype(f32), jnp.zeros((1, 128 - GROUPS), f32)], axis=1)
    scales = weights / jnp.sum(weights, axis=1, keepdims=True) * (128.0 * NP * nz / counts)
    own0 = lane_r == tab[3, 2 * me]
    own1 = lane_r == tab[3, 2 * me + 1]
    scale0 = jnp.sum(jnp.where(own0, scales, 0.0), axis=1, keepdims=True)
    scale1 = jnp.sum(jnp.where(own1, scales, 0.0), axis=1, keepdims=True)
    place_c = lax.broadcasted_iota(jnp.int32, (256, 1), 0)
    place_r = lax.broadcasted_iota(jnp.int32, (1, 256), 1)

    def valid_of(place):
        return jnp.where(place < 120, place < len0, place - 120 < len1)

    scale_c = jnp.where(place_c < 120, scale0, scale1)
    scale_r = jnp.where(place_r < 120, scale0, scale1)
    live_c = jnp.where(place_c < 120, jnp.where(place_c < len0, 1.0, 0.0), jnp.where(place_c - 120 < len1, 1.0, 0.0))
    live_r = jnp.where(place_r < 120, jnp.where(place_r < len0, 1.0, 0.0), jnp.where(place_r - 120 < len1, 1.0, 0.0))
    live_c2 = jnp.broadcast_to(live_c, (256, 128)) > 0.5
    live_r2 = jnp.broadcast_to(live_r, (128, 256)) > 0.5
    lane = lax.broadcasted_iota(jnp.int32, (256, 128), 1)
    key_place = lax.broadcasted_iota(jnp.int32, (256, 256), 0)
    query_place = lax.broadcasted_iota(jnp.int32, (256, 256), 1)
    bias = jnp.where(
        jnp.where(query_place < 120, key_place, keys0) < jnp.where(query_place < 120, keys0, key_place + 1),
        0.0, -1e30,
    ).astype(jnp.float32)
    nt = (((1,), (1,)), ((), ()))
    nn = (((1,), (0,)), ((), ()))

    def dot(a, b, dims):
        return lax.dot_general(a, b, dims, preferred_element_type=jnp.float32)

    def flat(ref, k):
        block = ref[k].astype(jnp.float32).reshape(240, 128)
        return jnp.concatenate([block, jnp.zeros((16, 128), jnp.float32)], axis=0)

    def d3(k):
        return pltpu.make_async_remote_copy(
            src_ref=sd.at[k],
            dst_ref=bq.at[pl.ds(me * PAIR, PAIR)],
            send_sem=s3,
            recv_sem=r3,
            device_id={"pack": back(k)},
            device_id_type=MESH,
        )

    def compute(k, loss):
        i = back(k)
        q = flat(qin, k)
        c = flat(cin, k)
        kb = kv[:, cols(i)]
        vb = vv[:, cols(i)]
        k_t = kb.T
        v_t = vb.T
        c_t = c.T
        u = jnp.where(live_c2, (c * scale_c).astype(jnp.bfloat16).astype(jnp.float32), 0.0)
        u_t = jnp.where(live_r2, (c_t * scale_r).astype(jnp.bfloat16).astype(jnp.float32), 0.0)
        dk = jnp.zeros((256, 128), jnp.float32)
        dv = jnp.zeros((256, 128), jnp.float32)
        dq_parts = []
        for h in range(2):
            own = (lane < 64) if h == 0 else (lane >= 64)
            q_h = jnp.where(own, q, 0.0).astype(jnp.bfloat16)
            u_h = jnp.where(own, u, 0.0).astype(jnp.bfloat16)
            scores = dot(kb, q_h, nt) + bias
            highest = jnp.max(scores, axis=0, keepdims=True)
            powers = jnp.exp(scores - highest)
            attention = powers * (1.0 / jnp.sum(powers, axis=0, keepdims=True))
            low = attention.astype(jnp.bfloat16)
            attended = dot(v_t[h * 64:(h + 1) * 64], low, nn).astype(jnp.bfloat16).astype(jnp.float32)
            loss = loss + jnp.sum(attended * c_t[h * 64:(h + 1) * 64], axis=0, keepdims=True)
            drift = jnp.sum(attended * u_t[h * 64:(h + 1) * 64], axis=0, keepdims=True)
            dv = dv + dot(low, u_h, nn)
            grad = dot(vb, u_h, nt)
            ds = (attention * (grad - drift)).astype(jnp.bfloat16)
            dq_parts.append(dot(k_t[h * 64:(h + 1) * 64], ds, nn))
            dk = dk + dot(ds, q_h, nn)
        dq = jnp.concatenate(dq_parts, axis=0).T
        dk_out[:, cols(i)] = dk.astype(jnp.bfloat16)
        dv_out[:, cols(i)] = dv.astype(jnp.bfloat16)
        sd_block = dq[:240].reshape(PAIR, 8, 128).astype(jnp.bfloat16)
        return sd_block, loss

    own_b = pltpu.make_async_copy(sd.at[0], bq.at[pl.ds(me * PAIR, PAIR)], lsem.at[6])

    def pair_step(k, loss):
        @pl.when(k > 0)
        def _():
            q2(k).wait_recv()
            c2(k).wait_recv()

        block, loss = compute(k, loss)
        sd[k] = block

        @pl.when(k > 0)
        def _():
            d3(k).start()

        @pl.when(k == 0)
        def _():
            own_b.start()

        return loss

    loss = lax.fori_loop(0, NP, pair_step, jnp.zeros((1, 256), jnp.float32))
    own_b.wait()
    loss = jnp.where(live_r > 0.5, loss, 0.0)
    loss0 = jnp.sum(jnp.where(place_r < 120, loss, 0.0), axis=1, keepdims=True)
    loss1 = jnp.sum(jnp.where(place_r < 120, 0.0, loss), axis=1, keepdims=True)
    own_loss = jnp.where(own0, loss0, 0.0) + jnp.where(own1, loss1, 0.0)
    lpart[me] = jnp.broadcast_to(own_loss, (8, 128))

    def loss_copy(k):
        return pltpu.make_async_remote_copy(
            src_ref=lpart.at[me],
            dst_ref=lpart.at[me],
            send_sem=sl,
            recv_sem=rl,
            device_id={"pack": peer(k)},
            device_id_type=MESH,
        )

    run(1, lambda k: loss_copy(k).start())

    all_d3 = total(bq.at[pl.ds(0, PAIR * (NP - 1))], s3, r3)
    all_d3.wait_recv()

    def d4(k):
        return pltpu.make_async_remote_copy(
            src_ref=dp.at[k],
            dst_ref=dq_out.at[:, :, cols(me)],
            send_sem=s4,
            recv_sem=r4,
            device_id={"pack": peer(k)},
            device_id_type=MESH,
        )

    own_d = pltpu.make_async_copy(dp.at[0], dq_out.at[:, :, cols(me)], lsem.at[4])

    def fill_d(k):
        d = peer(k)
        near = tab[4, 2 * d] * SLOT
        count = tab[5, 2 * d] // 8
        far = tab[4, 2 * d + 1] * SLOT - count
        for b in range(16):
            dp[k, b] = bq[jnp.clip(jnp.where(b < count, near, far) + b, 0, NP * PAIR - 1)]

    def send_d(k):
        fill_d(k)
        d4(k).start()

    run(1, send_d)
    fill_d(0)
    own_d.start()

    all_loss = total(lpart.at[pl.ds(0, NP - 1)], sl, rl)
    all_loss.wait_recv()
    lz[z] = jnp.sum(lpart[...], axis=0)

    all_zloss = total(lz.at[pl.ds(0, nz - 1)], szl, rzl)

    @pl.when(z == hub)
    def _():
        all_zloss.wait_recv()
        ltot[...] = jnp.sum(lz[...], axis=0)
        run_z(lambda k: from_hub(ltot, szm, rzm, k).start())

    @pl.when(z != hub)
    def _():
        to_hub(lz, szl, rzl).start()
        from_hub(ltot, szm, rzm, 1).wait_recv()

    mean_loss = ltot[:1] / counts
    loss_out[...] = mean_loss[:, :GROUPS]


    @pl.when(z == hub)
    def _():
        total(cnt.at[pl.ds(0, nz - 1)], szt, rzt).wait_send()
        total(lz.at[pl.ds(0, nz - 1)], szm, rzm).wait_send()

    @pl.when(z != hub)
    def _():
        to_hub(cnt, szc, rzc).wait_send()
        to_hub(lz, szl, rzl).wait_send()

    all_loss.wait_send()
    all_q1.wait_send()
    all_c1.wait_send()
    total(sq.at[pl.ds(0, NP - 1)], s2q, r2q.at[0]).wait_send()
    total(sc.at[pl.ds(0, NP - 1)], s2c, r2c.at[0]).wait_send()
    all_d3.wait_send()
    own_d.wait()
    total(dp.at[pl.ds(0, NP - 1)], s4, r4).wait_send()
    total(dp.at[pl.ds(0, NP - 1)], s4, r4).wait_recv()


def local(
    enc_keys, enc_values, dec_queries, cotangent,
    input_lengths, target_lengths, enc_pack, dec_pack, task_group, dro_weights,
):
    bf = jnp.bfloat16
    vmem = pl.BlockSpec(memory_space=pltpu.VMEM)
    hbm = pl.BlockSpec(memory_space=pl.ANY)
    nz = lax.axis_size("dp")
    dma = pltpu.SemaphoreType.DMA
    dq, dk, dv, loss = pl.pallas_call(
        kernel,
        out_shape=(
            pltpu.VMEM((16, 8, 4096), bf),
            pltpu.VMEM((256, 4096), bf),
            pltpu.VMEM((256, 4096), bf),
            pltpu.VMEM((1, GROUPS), jnp.float32),
        ),
        in_specs=[vmem] * 6 + [hbm] * 4,
        out_specs=(vmem, vmem, vmem, vmem),
        scratch_shapes=[
            pltpu.VMEM((256, 4096), bf),
            pltpu.VMEM((256, 4096), bf),
            pltpu.VMEM((TABLE + 16, 8, 128), bf),
            pltpu.VMEM((TABLE + 16, 8, 128), bf),
            pltpu.VMEM((NP, PAIR, 8, 128), bf),
            pltpu.VMEM((NP, PAIR, 8, 128), bf),
            pltpu.VMEM((NP, PAIR, 8, 128), bf),
            pltpu.VMEM((NP, PAIR, 8, 128), bf),
            pltpu.VMEM((NP, PAIR, 8, 128), bf),
            pltpu.VMEM((NP * PAIR + 16, 8, 128), bf),
            pltpu.VMEM((NP, 16, 8, 128), bf),
            pltpu.VMEM((8, 128), jnp.int32),
            pltpu.SMEM((8, 128), jnp.int32),
            pltpu.VMEM((nz, 8, 128), jnp.float32),
            pltpu.VMEM((NP, 8, 128), jnp.float32),
            pltpu.VMEM((nz, 8, 128), jnp.float32),
            pltpu.VMEM((8, 128), jnp.float32),
            pltpu.VMEM((8, 128), jnp.float32),
            dma((8,)),
            dma((20,)),
            dma((NP,)),
            dma((NP,)),
        ],
        compiler_params=pltpu.CompilerParams(
            collective_id=0, has_side_effects=True, vmem_limit_bytes=56 * 1024 * 1024
        ),
        cost_estimate=pl.CostEstimate(flops=3_000_000_000, bytes_accessed=11_000_000, transcendentals=4_000_000),
    )(
        input_lengths, target_lengths, enc_pack, dec_pack, task_group.reshape(1, 64), dro_weights.reshape(1, GROUPS),
        enc_keys, enc_values,
        dec_queries.reshape(16, 8, 4096), cotangent.reshape(16, 8, 4096),
    )
    return dq.reshape(128, 4096), dk, dv, loss.reshape(GROUPS)


def solution(mesh):
    rows = P(("dp", "pack"), None)
    small = P("dp", None)
    return jax.shard_map(
        local,
        mesh=mesh,
        in_specs=(rows, rows, rows, rows, small, small, small, small, P("dp", None, None), P()),
        out_specs=(rows, rows, rows, P()),
        check_vma=False,
    )
```
